256 devices in a mesh: grp: 4 (over x), dp: 64 (over y, z, core).
Axes of the slice: x: 4, y: 4, z: 8, core: 2. Of those that a mesh axis runs over, the one named last changes fastest.
Arguments:
- query_hidden: bfloat16 [32768, 4096], P(('grp', 'dp')), may hold values from -0.09375 to 0.09375
- passage_hidden: bfloat16 [32768, 4096], P(('grp', 'dp')), may hold values from -0.09375 to 0.09375
- gain: float32 [4096], replicated, may hold values from 0.1 to 1.9
- block_ids: int32 [256, 7], P(('grp', 'dp')), may hold values from 0 to 63, all different within a row
- positive_ids: int32 [32768], P(('grp', 'dp')), may hold values from 0 to 1407
Outputs:
- losses: float32 [32768], P(('grp', 'dp'))
- query_grad: bfloat16 [32768, 4096], P(('grp', 'dp'))
- passage_grad: bfloat16 [32768, 4096], P(('grp', 'dp'))
The draws below stay inside these ranges and needn't reach their ends.
Inputs may be any that keep to these rules, and one draw needn't show every extreme that they name: `block_ids`: each row names 7 different blocks.
All inputs are finite; a program needn't handle non-finite values.
Results may differ from the reference program's by a relative error of at most 0.01.
Values may be sent and summed in bfloat16 or wider, within the bound.
No kernel may reach another device: no remote copies, remote signals or barrier semaphores. Data moves between devices by JAX's collectives and lax.ppermute only.
A program may use at most 128 MiB of HBM per device.

```python
import jax
import jax.numpy as jnp
from jax import lax

D = 4096
QB = 128
PB = 128
HARD = 7
TOKENS = 32768
PASSAGES = 32768
COLUMNS = 1408
N_GRP = 4
N_DP = 64


def plant(array, own_key, least, largest):
    place = [jax.random.randint(jax.random.fold_in(own_key, axis), (), 0, length) for axis, length in enumerate(array.shape)]
    longest = array.shape.index(max(array.shape))
    next_to = place[:longest] + [(place[longest] + 1) % array.shape[longest]] + place[longest + 1:]
    return array.at[tuple(place)].set(least).at[tuple(next_to)].set(largest)


def levels(own_key, extent, split, smallest, largest):
    def one(dim, blocks):
        steps = jax.random.uniform(jax.random.fold_in(jax.random.fold_in(own_key, 6), dim), (blocks,), jnp.float32, smallest / len(split), largest / len(split))
        return jnp.repeat(jnp.exp(steps), extent[dim] // blocks).reshape((-1,) + (1,) * (len(extent) - dim - 1))

    level = one(*split[0])
    for cut in split[1:]:
        level = level * one(*cut)
    return level


def distinct(stream_key, rows, count, top, lift):
    order = jax.random.permutation(jax.random.fold_in(stream_key, 1), count)
    favour = order
    for power in range(3):
        favour = favour * favour // count
    favour = favour * lift // count
    tickets = jax.random.randint(jax.random.fold_in(stream_key, 2), (rows, count), 0, 4096) + favour
    fixed_rows = jax.random.permutation(jax.random.fold_in(stream_key, 3), rows)[jnp.arange(count) % rows]
    tickets = jnp.where(jnp.arange(rows)[:, None] == fixed_rows[None, :], 1 << 14, tickets)
    score = tickets * count + jnp.arange(count)
    return lax.top_k(score.astype(jnp.int32), top)[1].astype(jnp.int32)


def bell_draw(own_key, extent, deviation, reach, cuts=(), kind=jnp.bfloat16):
    drawn = deviation * jax.random.normal(own_key, extent, jnp.float32)
    if cuts:
        drawn = drawn * levels(own_key, extent, cuts, -0.22, 0.18)
    return jnp.clip(drawn, -reach, reach).astype(kind)


def setup_inputs(seed: int = 0) -> dict:
    streams_of = jax.random.split(jax.random.key(seed), 6)
    return {
        "query_hidden": bell_draw(streams_of[0], (TOKENS, D), 0.015625, 0.09375, ((0, 256),)),
        "passage_hidden": bell_draw(streams_of[1], (PASSAGES, D), 0.015625, 0.09375, ((0, 256),)),
        "gain": jnp.clip(1.0 + 0.18 * jax.random.normal(streams_of[2], (D,), jnp.float32), 0.1, 1.9),
        "block_ids": distinct(streams_of[3], (N_GRP * N_DP), N_DP, HARD, 1792),
        "positive_ids": plant(jax.random.randint(streams_of[4], (TOKENS,), 0, COLUMNS), jax.random.fold_in(streams_of[4], 1), 0, COLUMNS - 1).astype(jnp.int32),
    }


epsilon = 1e-06
score_scale = 50.0

def embed(hidden, gain):
    scaled = hidden.astype(jnp.float32) * gain
    norms = jnp.sqrt(lax.optimization_barrier(jnp.sum(scaled * scaled, axis=-1, keepdims=True)) + epsilon)
    return (scaled / norms, norms)

def unembed(unit, norms, grads, gain):
    inner = lax.optimization_barrier(jnp.sum(unit * grads, axis=-1, keepdims=True))
    return ((grads - unit * inner) / norms * gain).astype(jnp.bfloat16)

def reference(query_hidden, passage_hidden, gain, block_ids, positive_ids):
    devices = N_GRP * N_DP
    rows_block = PB // N_DP
    inside = N_GRP * PB
    query_f32, query_norms = embed(query_hidden, gain)
    query_unit = query_f32.astype(jnp.bfloat16)
    passage_f32, passage_norms = embed(passage_hidden, gain)
    passage_unit = passage_f32.astype(jnp.bfloat16)
    by_device = passage_unit.reshape(N_GRP, N_DP, PB, D)
    by_block = passage_unit.reshape(N_GRP, N_DP, N_DP, rows_block, D)
    queries_dev = query_unit.reshape(devices, QB, D)
    qf32_dev = query_f32.reshape(devices, QB, D)
    qnorm_dev = query_norms.reshape(devices, QB, 1)
    positive_dev = positive_ids.reshape(devices, QB)
    column_iota = jnp.arange(COLUMNS).astype(jnp.int32)
    group_iota = jnp.arange(N_GRP).astype(jnp.int32)
    source_iota = jnp.arange(N_DP).astype(jnp.int32)
    passage_iota = jnp.arange(PB).astype(jnp.int32)
    block_iota = jnp.arange(rows_block).astype(jnp.int32)

    def one_device(running, member):
        group_index = member // N_DP
        place_index = member % N_DP
        inbatch = jnp.take(by_device, place_index, axis=1).reshape(inside, D)
        chosen = jnp.take(block_ids, member, axis=0)
        column_blocks = jnp.take(by_block, group_index, axis=0)
        fetched = jnp.take(column_blocks, chosen, axis=1)
        fetched = jnp.transpose(fetched, (1, 0, 2, 3)).reshape(HARD * PB, D)
        candidates = jnp.concatenate([inbatch, fetched], axis=0)
        queries = jnp.take(queries_dev, member, axis=0)
        positive = jnp.take(positive_dev, member, axis=0)
        scores = score_scale * jnp.dot(queries, candidates.T, preferred_element_type=jnp.float32)
        powers = jnp.exp(scores)
        totals = lax.optimization_barrier(jnp.sum(powers, axis=1, keepdims=True))
        target = (column_iota[None, :] == positive[:, None]).astype(jnp.float32)
        losses = jnp.log(totals[:, 0]) - lax.optimization_barrier(jnp.sum(scores * target, axis=1))
        weights = (powers / totals - target).astype(jnp.bfloat16)
        unit_grad = score_scale * jnp.dot(weights, candidates, preferred_element_type=jnp.float32)
        candidate_grad = score_scale * jnp.dot(weights.T, queries, preferred_element_type=jnp.float32)
        inside_grad = candidate_grad[:inside]
        fetched_grad = lax.optimization_barrier(candidate_grad[inside:].astype(jnp.bfloat16)).astype(jnp.float32)
        inside_index = ((group_iota[:, None] * N_DP + place_index) * PB + passage_iota[None, :]).reshape(-1)
        fetched_index = ((group_index * N_DP + source_iota[None, :, None]) * PB + chosen[:, None, None] * rows_block + block_iota[None, None, :]).reshape(-1)
        running = running.at[inside_index].add(inside_grad)
        running = running.at[fetched_index].add(fetched_grad)
        query_out = unembed(jnp.take(qf32_dev, member, axis=0), jnp.take(qnorm_dev, member, axis=0), unit_grad, gain)
        return (running, (losses, query_out))
    running, (losses, query_grads) = lax.scan(one_device, jnp.zeros((PASSAGES, D), jnp.float32), jnp.arange(devices).astype(jnp.int32))
    passage_grad = unembed(passage_f32, passage_norms, running, gain)
    return (losses.reshape(TOKENS), query_grads.reshape(TOKENS, D), passage_grad)
```

```python
import jax
import jax.numpy as jnp
from jax import lax
from jax.sharding import Mesh, PartitionSpec as P

epsilon = 1e-06
score_scale = 50.0
halves = 2


def embed(hidden, gain):
    scaled = hidden.astype(jnp.float32) * gain
    norms = jnp.sqrt(jnp.sum(scaled * scaled, axis=-1, keepdims=True) + epsilon)
    return (scaled / norms, norms)


def unembed(unit, norms, grads, gain):
    inner = jnp.sum(unit * grads, axis=-1, keepdims=True)
    return ((grads - unit * inner) / norms * gain).astype(jnp.bfloat16)


def shift(value, axis, by):
    size = lax.axis_size(axis)
    return lax.ppermute(value, axis, [(i, (i + by) % size) for i in range(size)])


def ring_gather(own, axis):
    half = lax.axis_size(axis) // 2
    rows = own.shape[0] // 2
    blocks = {0: own}
    up = down = own
    for step in range(1, half):
        up, down = shift(up, axis, 1), shift(down, axis, -1)
        blocks[-step], blocks[step] = up, down
    blocks[half] = jnp.concatenate([shift(up[:rows], axis, 1), shift(down[rows:], axis, -1)], axis=0)
    return blocks


def ring_scatter(parts, axis):
    half = lax.axis_size(axis) // 2
    rows = parts[0].shape[0] // 2
    up = shift(parts[half][:rows].astype(jnp.bfloat16), axis, 1)
    down = shift(parts[half][rows:].astype(jnp.bfloat16), axis, -1)
    up = jnp.concatenate([parts[half - 1][:rows] + up, parts[half - 1][rows:]], axis=0)
    down = jnp.concatenate([parts[1 - half][:rows], parts[1 - half][rows:] + down], axis=0)
    for step in range(half - 1, 0, -1):
        up = shift(up.astype(jnp.bfloat16), axis, 1)
        down = shift(down.astype(jnp.bfloat16), axis, -1)
        if step > 1:
            up, down = parts[step - 1] + up, parts[1 - step] + down
    return parts[0] + up.astype(jnp.float32) + down.astype(jnp.float32)


def dot(a, b, dims):
    return lax.dot_general(a, b, (dims, ((), ())), preferred_element_type=jnp.float32)


def shards(query_hidden, passage_hidden, gain, block_ids, positive_ids):
    groups, n_y, n_z, n_c = (lax.axis_size(a) for a in ("x", "y", "z", "c"))
    i_y, i_z, i_c = (lax.axis_index(a) for a in ("y", "z", "c"))
    sources = n_y * n_z * n_c
    rows, width = query_hidden.shape
    rows_block = rows // sources
    inside = groups * rows
    z_order = list(range(1 - n_z // 2, n_z // 2 + 1))
    y_order = list(range(1 - n_y // 2, n_y // 2 + 1))

    ids = block_ids[0]
    extra = jnp.maximum(positive_ids - inside, 0)
    which, within = extra // rows, extra % rows
    block = jnp.sum(
        jnp.where(which[:, None] == jnp.arange(ids.shape[0])[None, :], ids[None, :], 0), axis=1
    )
    code = jnp.where(
        positive_ids < inside, -1, within // rows_block * rows + block * rows_block + within % rows_block
    )
    member = jnp.any(
        ids[:, None] == (jnp.arange(rows) // rows_block)[None, :], axis=0
    ).astype(jnp.int32)
    notes = jnp.stack([code, member])
    notes_all = lax.all_gather(notes, "z", axis=0)
    z_slots = (i_z + jnp.array(z_order)) % n_z
    notes_all = jnp.take(notes_all, z_slots, axis=0)
    codes, members = notes_all[:, 0], notes_all[:, 1] > 0

    query_f32, query_norms = embed(query_hidden, gain)
    query_unit = query_f32.astype(jnp.bfloat16)
    passage_f32, passage_norms = embed(passage_hidden, gain)
    passage_unit = passage_f32.astype(jnp.bfloat16)

    part = rows // halves
    query_parts = []
    for h in range(halves):
        blocks = ring_gather(query_unit[h * part : (h + 1) * part], "z")
        query_parts.append(jnp.concatenate([blocks[k] for k in z_order], axis=0))
    column = ring_gather(passage_unit, "y")
    column = jnp.concatenate([column[k] for k in y_order], axis=0)
    passages = jnp.concatenate([column, shift(column, "c", 1)], axis=0)
    c_slots = jnp.stack([i_c, 1 - i_c])
    y_slots = (i_y + jnp.array(y_order)) % n_y
    slot_source = ((y_slots[None, :] * n_z + i_z) * n_c + c_slots[:, None]).reshape(-1)
    passage_code = (slot_source[:, None] * rows + jnp.arange(rows)[None, :]).reshape(-1)

    inbatch = lax.all_gather(passage_unit, "x", axis=0, tiled=True)
    scores_in = score_scale * dot(query_unit, inbatch, ((1,), (1,)))
    target_in = jnp.arange(inside)[None, :] == positive_ids[:, None]
    powers_in = jnp.exp(scores_in)
    own_sums = jnp.stack(
        [jnp.sum(powers_in, axis=1), jnp.sum(jnp.where(target_in, scores_in, 0.0), axis=1)]
    )

    fetched, totals_own, query_grads = [], [], []
    passage_part = 0.0
    for h in range(halves):
        span = slice(h * part, (h + 1) * part)
        queries = query_parts[h]
        scores = score_scale * dot(queries, passages, ((1,), (1,)))
        mask = jnp.tile(jnp.repeat(members, part, axis=0), (1, n_y * n_c))
        target = codes[:, span].reshape(-1)[:, None] == passage_code[None, :]
        powers = jnp.where(mask, jnp.exp(scores), 0.0)
        sums = jnp.stack(
            [jnp.sum(powers, axis=1), jnp.sum(jnp.where(target, scores, 0.0), axis=1)]
        ).reshape(2, n_z, part)
        own = z_order.index(0)
        sums = sums.at[:, own].add(own_sums[:, span])
        place = (jnp.arange(n_z)[:, None] == z_slots[None, :]).astype(jnp.float32)
        sums = jnp.sum(place[None, :, :, None] * sums[:, None], axis=2)
        sums = lax.psum(sums, "z")
        sums = jnp.sum(place.T[None, :, :, None] * sums[:, None], axis=2)
        totals_own.append(sums[:, own])
        totals = sums[0].reshape(-1, 1)
        weights = (powers / totals - target.astype(jnp.float32)).astype(jnp.bfloat16)
        grads = dot(weights, passages, ((1,), (0,))).reshape(n_z, part, width)
        query_grads.append(
            ring_scatter({k: grads[j] for j, k in enumerate(z_order)}, "z")
        )
        passage_part += dot(weights, queries, ((0,), (0,)))
    sums = jnp.concatenate(totals_own, axis=1)
    losses = jnp.log(sums[0]) - sums[1]
    weights_in = (powers_in / sums[0][:, None] - target_in.astype(jnp.float32)).astype(jnp.bfloat16)
    query_grad_in = dot(weights_in, inbatch, ((1,), (0,)))
    own_grad = lax.psum_scatter(
        dot(weights_in, query_unit, ((0,), (0,))).astype(jnp.bfloat16),
        "x",
        scatter_dimension=0,
        tiled=True,
    ).astype(jnp.float32)

    passage_part = passage_part.reshape(n_c, n_y, rows, width)
    other = shift(passage_part[1].astype(jnp.bfloat16), "c", 1)
    passage_part = passage_part[0] + other.astype(jnp.float32)
    fetched_sum = ring_scatter({k: passage_part[j] for j, k in enumerate(y_order)}, "y")

    passage_grad = unembed(
        passage_f32, passage_norms, score_scale * (own_grad + fetched_sum), gain
    )
    query_grad = unembed(
        query_f32,
        query_norms,
        score_scale * (jnp.concatenate(query_grads, axis=0) + query_grad_in),
        gain,
    )
    return (losses, query_grad, passage_grad)


def solution(mesh):
    split = Mesh(mesh.devices.reshape(4, 4, 8, 2), ("x", "y", "z", "c"))
    whole = ("x", "y", "z", "c")
    return jax.shard_map(
        shards,
        mesh=split,
        in_specs=(P(whole, None), P(whole, None), P(), P(whole, None), P(whole)),
        out_specs=(P(whole), P(whole, None), P(whole, None)),
        check_vma=False,
    )
```

```python
import jax
import jax.numpy as jnp
from jax import lax
from jax.experimental import pallas as pl
from jax.experimental.pallas import tpu as pltpu
from jax.sharding import Mesh, PartitionSpec as P

epsilon = 1e-06
score_scale = 50.0


def embed_kernel(hidden_ref, gain_ref, unit_ref, norm_ref):
    scaled = hidden_ref[...].astype(jnp.float32) * gain_ref[...]
    norm = jnp.sqrt(jnp.sum(scaled * scaled, axis=-1, keepdims=True) + epsilon)
    unit_ref[...] = (scaled * (1.0 / norm)).astype(jnp.bfloat16)
    norm_ref[...] = norm


def embed(hidden, gain):
    rows, width = hidden.shape
    block = rows // 2
    tile = pl.BlockSpec((block, width), lambda i: (i, 0))
    return pl.pallas_call(
        embed_kernel,
        grid=(rows // block,),
        in_specs=[tile, pl.BlockSpec((1, width), lambda i: (0, 0))],
        out_specs=[tile, pl.BlockSpec((block, 1), lambda i: (i, 0))],
        out_shape=[
            jax.ShapeDtypeStruct((rows, width), jnp.bfloat16),
            jax.ShapeDtypeStruct((rows, 1), jnp.float32),
        ],
        cost_estimate=pl.CostEstimate(
            flops=4 * rows * width, bytes_accessed=4 * rows * width, transcendentals=0
        ),
    )(hidden, gain[None, :])


def unembed_kernel(hidden_ref, gain_ref, norm_ref, *refs):
    out_ref = refs[-1]
    grads = refs[0][...].astype(jnp.float32)
    for ref in refs[1:-1]:
        grads += ref[...].astype(jnp.float32)
    grads = score_scale * grads
    gain, inverse = gain_ref[...], 1.0 / norm_ref[...]
    unit = hidden_ref[...].astype(jnp.float32) * gain * inverse
    inner = jnp.sum(unit * grads, axis=-1, keepdims=True)
    out_ref[...] = ((grads - unit * inner) * inverse * gain).astype(jnp.bfloat16)


def unembed(hidden, gain, norms, terms):
    rows, width = hidden.shape
    block = rows // 4
    tile = pl.BlockSpec((block, width), lambda i: (i, 0))
    return pl.pallas_call(
        unembed_kernel,
        grid=(rows // block,),
        in_specs=[
            tile,
            pl.BlockSpec((1, width), lambda i: (0, 0)),
            pl.BlockSpec((block, 1), lambda i: (i, 0)),
        ]
        + [tile] * len(terms),
        out_specs=tile,
        out_shape=jax.ShapeDtypeStruct((rows, width), jnp.bfloat16),
        cost_estimate=pl.CostEstimate(
            flops=8 * rows * width, bytes_accessed=8 * rows * width, transcendentals=0
        ),
    )(hidden, gain[None, :], norms, *terms)


def gated_kernel(value_ref, *refs):
    refs[-1][...] = value_ref[...]


def gated(value, *others):
    return pl.pallas_call(
        gated_kernel,
        in_specs=[pl.BlockSpec(memory_space=pltpu.VMEM)]
        + [pl.BlockSpec(memory_space=pl.ANY)] * len(others),
        out_specs=pl.BlockSpec(memory_space=pltpu.VMEM),
        out_shape=jax.ShapeDtypeStruct(value.shape, value.dtype),
    )(value, *others)


def scores_kernel(count, slots_ref, query_ref, code_ref, member_ref, sums_ref, *refs):
    passages, powers_ref, out_ref = refs[:count], refs[count], refs[count + 1]
    rows = passages[0].shape[0]
    queries = query_ref[...]
    code = code_ref[...]
    blocks = member_ref.shape[0]
    mask = jnp.broadcast_to(member_ref[...], (blocks, rows, rows)).reshape(blocks * rows, rows) > 0
    total, target_score = sums_ref[:, 0:1], sums_ref[:, 1:2]
    column = lax.broadcasted_iota(jnp.int32, (1, rows), 1)
    for j, ref in enumerate(passages):
        scores = score_scale * lax.dot_general(
            queries, ref[...], (((1,), (1,)), ((), ())), preferred_element_type=jnp.float32
        )
        powers = jnp.where(mask, jnp.exp(scores), 0.0)
        target = code == column + slots_ref[j] * rows
        powers_ref[:, j * rows : (j + 1) * rows] = powers
        total = total + jnp.sum(powers, axis=1, keepdims=True)
        target_score = target_score + jnp.sum(
            jnp.where(target, scores, 0.0), axis=1, keepdims=True
        )
    out_ref[:, 0:1] = total
    out_ref[:, 1:2] = target_score


def score(queries, codes, members, sums, slots, passages):
    total, width = queries.shape
    rows = passages[0].shape[0]
    tile, count = 4 * rows, len(passages)
    return pl.pallas_call(
        lambda *refs: scores_kernel(count, *refs),
        grid=(total // tile,),
        in_specs=[
            pl.BlockSpec(memory_space=pltpu.SMEM),
            pl.BlockSpec((tile, width), lambda i: (i, 0)),
            pl.BlockSpec((tile, 1), lambda i: (i, 0)),
            pl.BlockSpec((tile // rows, 1, rows), lambda i: (i, 0, 0)),
            pl.BlockSpec((tile, 2), lambda i: (i, 0)),
        ]
        + [pl.BlockSpec((rows, width), lambda i: (0, 0))] * count,
        out_specs=[
            pl.BlockSpec((tile, count * rows), lambda i: (i, 0)),
            pl.BlockSpec((tile, 2), lambda i: (i, 0)),
        ],
        out_shape=[
            jax.ShapeDtypeStruct((total, count * rows), jnp.float32),
            jax.ShapeDtypeStruct((total, 2), jnp.float32),
        ],
        compiler_params=pltpu.CompilerParams(vmem_limit_bytes=28 * 1024 * 1024),
        cost_estimate=pl.CostEstimate(
            flops=2 * total * count * rows * width,
            bytes_accessed=2 * (total + count * rows) * width,
            transcendentals=total * count * rows,
        ),
    )(slots, queries, codes, members, sums, *passages)


def shift(value, axis, by):
    size = lax.axis_size(axis)
    return lax.ppermute(value, axis, [(i, (i + by) % size) for i in range(size)])


def offsets(size):
    far = size // 2
    return [far] + [s * k for k in range(far - 1, 0, -1) for s in (1, -1)] + [0]


def sum_over(value, axis, order, dim):
    size = lax.axis_size(axis)
    place = {k % size: j for j, k in enumerate(order)}
    by = size // 2
    while by:
        other = shift(value, axis, -by)
        moved = [
            lax.index_in_dim(other, place[(k - by) % size], dim, keepdims=True) for k in order
        ]
        value = value + jnp.concatenate(moved, axis=dim)
        by //= 2
    return value


def ring_gather(own, axis, cut):
    half = lax.axis_size(axis) // 2
    blocks = {0: own}
    up = down = own
    for step in range(1, half):
        up, down = shift(up, axis, 1), shift(down, axis, -1)
        blocks[-step], blocks[step] = up, down
    blocks[half] = jnp.concatenate([shift(up[:cut], axis, 1), shift(down[cut:], axis, -1)], axis=0)
    return blocks


def ring_scatter(terms, axis):
    half = lax.axis_size(axis) // 2
    far = terms[half]().astype(jnp.bfloat16)
    rows = far.shape[0] // 2
    up, down = shift(far[:rows], axis, 1), shift(far[rows:], axis, -1)
    for step in range(half - 1, 0, -1):
        above, below = terms[step](up), terms[-step](up)
        if step == half - 1:
            up = jnp.concatenate([above[:rows] + up, above[rows:]], axis=0)
            down = jnp.concatenate([below[:rows], below[rows:] + down], axis=0)
        else:
            up, down = above + up, below + down
        up = shift(up.astype(jnp.bfloat16), axis, 1)
        down = shift(down.astype(jnp.bfloat16), axis, -1)
    return terms[0](), up, down


def dot(a, b, dims):
    return lax.dot_general(a, b, (dims, ((), ())), preferred_element_type=jnp.float32)


def shards(query_hidden, passage_hidden, gain, block_ids, positive_ids):
    groups, n_y, n_z, n_c = (lax.axis_size(a) for a in ("x", "y", "z", "c"))
    i_x, i_y, i_z, i_c = (lax.axis_index(a) for a in ("x", "y", "z", "c"))
    sources = n_y * n_z * n_c
    rows, width = query_hidden.shape
    rows_block = rows // sources
    inside = groups * rows
    x_order, y_order, z_order = offsets(groups), offsets(n_y), offsets(n_z)
    blocks = n_c * n_y
    own = n_y - 1
    low = 64

    passage_unit, passage_norms = embed(passage_hidden, gain)
    column = ring_gather(passage_unit, "z", rows // 2)

    ids = block_ids[0]
    extra = jnp.maximum(positive_ids - inside, 0)
    which, within = extra // rows, extra % rows
    block = jnp.sum(
        jnp.where(which[:, None] == jnp.arange(ids.shape[0])[None, :], ids[None, :], 0), axis=1
    )
    code = within // rows_block * rows + block * rows_block + within % rows_block
    member = jnp.any(ids[:, None] == (jnp.arange(rows) // rows_block)[None, :], axis=0)
    notes = jnp.stack(
        [jnp.where(positive_ids < inside, -1, code // low), code % low, member.astype(jnp.int32)]
    ).astype(jnp.bfloat16)
    notes = jnp.pad(notes, ((0, 13), (0, width - rows)))

    query_unit, query_norms = embed(query_hidden, gain)
    row = ring_gather(jnp.concatenate([query_unit, notes], axis=0), "y", rows // 2)
    row = [row[k] for k in y_order]
    row = row + [shift(b, "c", 1) for b in row]
    queries = jnp.concatenate([b[:rows] for b in row], axis=0)
    notes = jnp.stack([b[rows : rows + 3, :rows] for b in row]).astype(jnp.int32)
    codes = (notes[:, 0] * low + notes[:, 1]).reshape(blocks * rows, 1)
    members = notes[:, 2:3].astype(jnp.float32)

    inbatch = ring_gather(gated(passage_unit, row[0]), "x", rows // 2)
    inbatch = jnp.concatenate([inbatch[k] for k in x_order], axis=0)
    x_slots = (i_x + jnp.array(x_order)) % groups
    inbatch_code = (x_slots[:, None] * rows + jnp.arange(rows)[None, :]).reshape(-1)
    scores_in = score_scale * dot(query_unit, inbatch, ((1,), (1,)))
    target_in = inbatch_code[None, :] == positive_ids[:, None]
    powers_in = jnp.exp(scores_in)
    own_sums = jnp.stack(
        [jnp.sum(powers_in, axis=1), jnp.sum(jnp.where(target_in, scores_in, 0.0), axis=1)], axis=1
    )

    arrivals = [[0, 1, -1]] + [[k, -k] for k in range(2, n_z // 2)] + [[n_z // 2]]
    sums = jnp.zeros((blocks * rows, 2), jnp.float32)
    powers, targets = {}, {}
    for offs in arrivals:
        if offs == arrivals[-1]:
            sums = sums + jnp.pad(own_sums, ((own * rows, (blocks - 1 - own) * rows), (0, 0)))
        slots = (i_y * n_z + (i_z + jnp.array(offs)) % n_z) * n_c + i_c
        got, sums = score(queries, codes, members, sums, slots, [column[k] for k in offs])
        for j, k in enumerate(offs):
            powers[k] = got[:, j * rows : (j + 1) * rows]
            col_code = slots[j] * rows + jnp.arange(rows)
            targets[k] = (codes == col_code[None, :]).astype(jnp.float32)
    sums = sums.T.reshape(2, n_c, n_y, rows)
    sums = sums + shift(sums, "c", 1)[:, ::-1]
    sums = sum_over(sums, "y", y_order, 2).reshape(2, blocks * rows)
    scale = 1.0 / sums[0][:, None]

    def weigh(offs, by):
        out = jnp.concatenate([powers[k] * by - targets[k] for k in offs], axis=1)
        return lax.optimization_barrier(out.astype(jnp.bfloat16))

    kept = {}

    def term(k):
        def of(*arrived):
            group = [0] if k == 0 else [n_z // 2] if k == n_z // 2 else [abs(k), -abs(k)]
            if k in kept:
                return kept.pop(k)
            by = scale
            if abs(k) <= 1:
                by = later[1]
            elif abs(k) == 2:
                by = later[0]
            got = dot(weigh(group, by), queries, ((0,), (0,))).reshape(len(group), rows, width)
            for j, g in enumerate(group):
                kept[g] = got[j]
            return kept.pop(k)

        def run(*arrived):
            if arrived and len(later) < 2 and abs(k) < n_z // 2 and k > 0:
                later.append(gated(scale, *arrived))
            return of(*arrived)

        return run

    later = []
    fetched_terms = ring_scatter({k: term(k) for k in z_order}, "z")

    own_sums = sums[:, own * rows : (own + 1) * rows]
    losses = jnp.log(own_sums[0]) - own_sums[1]
    scale_in = 1.0 / own_sums[0][:, None]
    weights_in = lax.optimization_barrier(
        (powers_in * scale_in - target_in.astype(jnp.float32)).astype(jnp.bfloat16)
    )
    query_grad_in = dot(weights_in, inbatch, ((1,), (0,)))
    inside_grad = {
        k: dot(weights_in[:, j * rows : (j + 1) * rows], query_unit, ((0,), (0,)))
        for j, k in enumerate(x_order)
    }
    inside_terms = ring_scatter({k: (lambda *_, k=k: inside_grad[k]) for k in x_order}, "x")

    passages = jnp.concatenate([column[k] for k in z_order], axis=0)
    half = n_y * rows
    there = weigh(z_order, later[0])[half:]
    here = weigh(z_order, later[1])[:half]
    query_part = dot(here, passages, ((1,), (0,))) + shift(
        dot(there, passages, ((1,), (0,))).astype(jnp.bfloat16), "c", 1
    ).astype(jnp.float32)
    query_part = query_part.reshape(n_y, rows, width)
    query_terms = ring_scatter(
        {k: (lambda *_, j=j: query_part[j]) for j, k in enumerate(y_order)}, "y"
    )

    query_grad = unembed(query_hidden, gain, query_norms, (*query_terms, query_grad_in))
    passage_grad = unembed(passage_hidden, gain, passage_norms, (*fetched_terms, *inside_terms))
    return (losses, query_grad, passage_grad)


def solution(mesh):
    split = Mesh(mesh.devices.reshape(4, 4, 8, 2), ("x", "y", "z", "c"))
    whole = ("x", "y", "z", "c")
    return jax.shard_map(
        shards,
        mesh=split,
        in_specs=(P(whole, None), P(whole, None), P(), P(whole, None), P(whole)),
        out_specs=(P(whole), P(whole, None), P(whole, None)),
        check_vma=False,
    )
```

```python
import jax
import jax.numpy as jnp
from jax import lax
from jax.experimental import pallas as pl
from jax.experimental.pallas import tpu as pltpu
from jax.sharding import Mesh, PartitionSpec as P

epsilon = 1e-06
score_scale = 50.0


chunk = 512


def pieces(width):
    return [pl.ds(i, chunk) for i in range(0, width, chunk)]


def fold(value):
    out = value[:, :128]
    for i in range(128, value.shape[1], 128):
        out += value[:, i : i + 128]
    return out


def unit_rows(hidden_ref, gain_ref, part, unit_ref, norm_ref):
    count, width = part.size, hidden_ref.shape[1]
    square = jnp.zeros((count, 128), jnp.float32)
    for at in pieces(width):
        scaled = hidden_ref[part, at].astype(jnp.float32) * gain_ref[:, at]
        square += fold(scaled * scaled)
    norm = jnp.sqrt(jnp.sum(square, axis=-1, keepdims=True) + epsilon)
    inverse = 1.0 / norm
    for at in pieces(width):
        scaled = hidden_ref[part, at].astype(jnp.float32) * gain_ref[:, at]
        unit_ref[part, at] = (scaled * inverse).astype(jnp.bfloat16)
    norm_ref[part, :] = norm


def embed_kernel(hidden_ref, gain_ref, unit_ref, norm_ref):
    unit_rows(hidden_ref, gain_ref, pl.ds(0, hidden_ref.shape[0]), unit_ref, norm_ref)


def embed(hidden, gain):
    rows, width = hidden.shape
    block = rows // 4
    tile = pl.BlockSpec((block, width), lambda i: (i, 0))
    return pl.pallas_call(
        embed_kernel,
        grid=(rows // block,),
        in_specs=[tile, pl.BlockSpec((1, width), lambda i: (0, 0))],
        out_specs=[tile, pl.BlockSpec((block, 1), lambda i: (i, 0))],
        out_shape=[
            jax.ShapeDtypeStruct((rows, width), jnp.bfloat16),
            jax.ShapeDtypeStruct((rows, 1), jnp.float32),
        ],
        cost_estimate=pl.CostEstimate(
            flops=4 * rows * width, bytes_accessed=4 * rows * width, transcendentals=0
        ),
    )(hidden, gain[None, :])


low = 64
note_rows = 16


def embed_noted_kernel(
    inside, rows_block, ids_ref, positive_ref, hidden_ref, gain_ref, other_ref, unit_ref, norm_ref
):
    del other_ref
    rows, width = hidden_ref.shape
    for first in range(0, rows, 32):
        unit_rows(hidden_ref, gain_ref, pl.ds(first, 32), unit_ref, norm_ref)
    positive = jnp.broadcast_to(positive_ref[...], (note_rows, rows))
    extra = jnp.maximum(positive - inside, 0)
    which, within = extra // rows, extra % rows
    lane_block = lax.broadcasted_iota(jnp.int32, (note_rows, rows), 1) // rows_block
    block = jnp.zeros((note_rows, rows), jnp.int32)
    member = jnp.zeros((note_rows, rows), jnp.int32)
    for k in range(ids_ref.shape[1]):
        block = jnp.where(which == k, ids_ref[0, k], block)
        member = jnp.where(lane_block == ids_ref[0, k], 1, member)
    code = within // rows_block * rows + block * rows_block + within % rows_block
    kind = lax.broadcasted_iota(jnp.int32, (note_rows, rows), 0)
    notes = jnp.where(kind == 0, jnp.where(positive < inside, -1, code // low), 0)
    notes = jnp.where(kind == 1, code % low, jnp.where(kind == 2, member, notes))
    unit_ref[pl.ds(rows, note_rows), :] = jnp.zeros((note_rows, width), jnp.bfloat16)
    unit_ref[pl.ds(rows, note_rows), pl.ds(0, rows)] = notes.astype(jnp.float32).astype(jnp.bfloat16)


def embed_noted(hidden, gain, ids, positive, inside, rows_block, other):
    rows, width = hidden.shape
    vmem = pl.BlockSpec(memory_space=pltpu.VMEM)
    return pl.pallas_call(
        lambda *refs: embed_noted_kernel(inside, rows_block, *refs),
        in_specs=[pl.BlockSpec(memory_space=pltpu.SMEM)]
        + [vmem] * 3
        + [pl.BlockSpec(memory_space=pl.ANY)],
        out_specs=[vmem, vmem],
        out_shape=[
            jax.ShapeDtypeStruct((rows + note_rows, width), jnp.bfloat16),
            jax.ShapeDtypeStruct((rows, 1), jnp.float32),
        ],
        cost_estimate=pl.CostEstimate(
            flops=4 * rows * width, bytes_accessed=4 * rows * width, transcendentals=0
        ),
    )(ids, positive[None, :], hidden, gain[None, :], other)


def unembed_kernel(hidden_ref, gain_ref, norm_ref, *refs):
    terms, out_ref, kept_ref = refs[:-2], refs[-2], refs[-1]
    rows, width = hidden_ref.shape
    inverse = 1.0 / norm_ref[...]
    inner = jnp.zeros((rows, 128), jnp.float32)
    for at in pieces(width):
        grads = jnp.zeros((rows, chunk), jnp.float32)
        for ref in terms:
            if len(ref.shape) == 3:
                for j in range(ref.shape[0]):
                    grads += ref[j, :, at].astype(jnp.float32)
            else:
                grads += ref[:, at].astype(jnp.float32)
        kept_ref[:, at] = grads
        unit = hidden_ref[:, at].astype(jnp.float32) * gain_ref[:, at]
        inner += fold(unit * grads)
    inner = jnp.sum(inner, axis=-1, keepdims=True) * inverse
    for at in pieces(width):
        unit = hidden_ref[:, at].astype(jnp.float32) * gain_ref[:, at] * inverse
        grads = kept_ref[:, at] - unit * inner
        out_ref[:, at] = (grads * (score_scale * inverse) * gain_ref[:, at]).astype(jnp.bfloat16)


def unembed(hidden, gain, norms, terms):
    rows, width = hidden.shape
    block = rows // 4
    tile = pl.BlockSpec((block, width), lambda i: (i, 0))
    return pl.pallas_call(
        unembed_kernel,
        grid=(rows // block,),
        in_specs=[
            tile,
            pl.BlockSpec((1, width), lambda i: (0, 0)),
            pl.BlockSpec((block, 1), lambda i: (i, 0)),
        ]
        + [
            tile
            if len(term.shape) == 2
            else pl.BlockSpec((term.shape[0], block, width), lambda i: (0, i, 0))
            for term in terms
        ],
        out_specs=tile,
        out_shape=jax.ShapeDtypeStruct((rows, width), jnp.bfloat16),
        scratch_shapes=[pltpu.VMEM((block, width), jnp.float32)],
        cost_estimate=pl.CostEstimate(
            flops=8 * rows * width, bytes_accessed=8 * rows * width, transcendentals=0
        ),
    )(hidden, gain[None, :], norms, *terms)


def gated_kernel(value_ref, *refs):
    refs[-1][...] = value_ref[...]


def gated(value, *others):
    return pl.pallas_call(
        gated_kernel,
        in_specs=[pl.BlockSpec(memory_space=pltpu.VMEM)]
        + [pl.BlockSpec(memory_space=pl.ANY)] * len(others),
        out_specs=pl.BlockSpec(memory_space=pltpu.VMEM),
        out_shape=jax.ShapeDtypeStruct(value.shape, value.dtype),
    )(value, *others)


def shift(value, axis, by):
    size = lax.axis_size(axis)
    return lax.ppermute(value, axis, [(i, (i + by) % size) for i in range(size)])


def offsets(size):
    far = size // 2
    return [far] + [s * k for k in range(far - 1, 0, -1) for s in (1, -1)] + [0]


def sum_over(value, axis, order, dim):
    size = lax.axis_size(axis)
    place = {k % size: j for j, k in enumerate(order)}
    by = size // 2
    while by:
        other = shift(value, axis, -by)
        moved = [
            lax.index_in_dim(other, place[(k - by) % size], dim, keepdims=True) for k in order
        ]
        value = value + jnp.concatenate(moved, axis=dim)
        by //= 2
    return value


def ring_gather(own, axis, cut):
    half = lax.axis_size(axis) // 2
    blocks = {0: own}
    up = down = own
    for step in range(1, half):
        up, down = shift(up, axis, 1), shift(down, axis, -1)
        blocks[-step], blocks[step] = up, down
    blocks[half] = jnp.concatenate([shift(up[:cut], axis, 1), shift(down[cut:], axis, -1)], axis=0)
    return blocks


def ring_scatter(terms, axis):
    half = lax.axis_size(axis) // 2
    arrived = []
    far = terms[half](arrived).astype(jnp.bfloat16)
    rows = far.shape[0] // 2
    up, down = shift(far[:rows], axis, 1), shift(far[rows:], axis, -1)
    for step in range(half - 1, 0, -1):
        arrived.append((up, down))
        above, below = (terms[k](arrived).astype(jnp.float32) for k in (step, -step))
        if step == half - 1:
            up = jnp.concatenate([above[:rows] + up, above[rows:]], axis=0)
            down = jnp.concatenate([below[:rows], below[rows:] + down], axis=0)
        else:
            up, down = above + up, below + down
        up = shift(up.astype(jnp.bfloat16), axis, 1)
        down = shift(down.astype(jnp.bfloat16), axis, -1)
    return terms[0](arrived), up, down


def dot(a, b, dims, kind=jnp.float32):
    return lax.dot_general(a, b, (dims, ((), ())), preferred_element_type=jnp.float32).astype(kind)


def shards(query_hidden, passage_hidden, gain, block_ids, positive_ids):
    groups, n_y, n_z, n_c = (lax.axis_size(a) for a in ("x", "y", "z", "c"))
    i_x, i_y, i_c = (lax.axis_index(a) for a in ("x", "y", "c"))
    sources = n_y * n_z * n_c
    rows, width = query_hidden.shape
    rows_block = rows // sources
    inside = groups * rows
    x_order, y_order = offsets(groups), offsets(n_y)
    blocks = n_c * n_y
    own = n_y - 1

    passage_unit, passage_norms = embed(passage_hidden, gain)
    passages = lax.all_gather(passage_unit, "z", axis=0, tiled=True)
    slots = (i_y * n_z + jnp.arange(n_z)) * n_c + i_c
    passage_code = (slots[:, None] * rows + jnp.arange(rows)[None, :]).reshape(-1)

    noted, query_norms = embed_noted(
        query_hidden, gain, block_ids, positive_ids, inside, rows_block, passage_norms
    )
    row = ring_gather(noted, "y", rows // 2)
    row = [row[k] for k in y_order]
    row = row + [shift(b, "c", 1) for b in row]
    query_unit = noted[:rows]
    queries = jnp.concatenate([b[:rows] for b in row], axis=0)
    notes = jnp.stack([b[rows : rows + 3, :rows] for b in row]).astype(jnp.int32)
    codes = (notes[:, 0] * low + notes[:, 1]).reshape(blocks * rows, 1)
    members = jnp.repeat(notes[:, 2] > 0, rows, axis=0)

    inbatch = ring_gather(passage_unit, "x", rows // 2)
    inbatch = jnp.concatenate([inbatch[k] for k in x_order], axis=0)
    x_slots = (i_x + jnp.array(x_order)) % groups
    inbatch_code = (x_slots[:, None] * rows + jnp.arange(rows)[None, :]).reshape(-1)
    scores_in = score_scale * dot(query_unit, inbatch, ((1,), (1,)))
    target_in = inbatch_code[None, :] == positive_ids[:, None]
    powers_in = jnp.exp(scores_in)
    own_sums = jnp.stack(
        [jnp.sum(powers_in, axis=1), jnp.sum(jnp.where(target_in, scores_in, 0.0), axis=1)]
    )

    scores = score_scale * dot(queries, passages, ((1,), (1,)))
    target = codes == passage_code[None, :]
    powers = jnp.where(jnp.tile(members, (1, n_z)), jnp.exp(scores), 0.0)
    sums = jnp.stack([jnp.sum(powers, axis=1), jnp.sum(jnp.where(target, scores, 0.0), axis=1)])
    sums = sums + jnp.pad(own_sums, ((0, 0), (own * rows, (blocks - 1 - own) * rows)))
    sums = sums.reshape(2, n_c, n_y, rows)
    sums = sums + shift(sums, "c", 1)[:, ::-1]
    sums = sum_over(sums, "y", y_order, 2).reshape(2, blocks * rows)
    scale = 1.0 / sums[:1]

    def weigh(by):
        out = powers * by[0][:, None] - target.astype(jnp.float32)
        return lax.optimization_barrier(out.astype(jnp.bfloat16))

    passage_part = dot(weigh(scale), queries, ((0,), (0,)), jnp.bfloat16)
    fetched = lax.psum_scatter(passage_part, "z", scatter_dimension=0, tiled=True)

    half = n_y * rows
    weights = weigh(gated(scale, passage_part))
    there = shift(dot(weights[half:], passages, ((1,), (0,)), jnp.bfloat16), "c", 1)
    here = dot(weights[:half], passages, ((1,), (0,))) + there.astype(jnp.float32)
    here = here.astype(jnp.bfloat16).reshape(n_y, rows, width)
    query_terms = ring_scatter({k: (lambda _, j=j: here[j]) for j, k in enumerate(y_order)}, "y")

    own_sums = sums[:, own * rows : (own + 1) * rows]
    losses = jnp.log(own_sums[0]) - own_sums[1]
    scale_in = gated(1.0 / own_sums[:1], passage_part)[0]
    weights_in = lax.optimization_barrier(
        (powers_in * scale_in[:, None] - target_in.astype(jnp.float32)).astype(jnp.bfloat16)
    )
    inside_grad = dot(weights_in, query_unit, ((0,), (0,)), jnp.bfloat16)
    inside_grad = inside_grad.reshape(groups, rows, width)
    inside_terms = ring_scatter(
        {k: (lambda _, j=j: inside_grad[j]) for j, k in enumerate(x_order)}, "x"
    )
    inside_query = dot(weights_in, inbatch, ((1,), (0,)))

    query_grad = unembed(query_hidden, gain, query_norms, (*query_terms, inside_query))
    passage_grad = unembed(passage_hidden, gain, passage_norms, (*inside_terms, fetched))
    return (losses, query_grad, passage_grad)


def solution(mesh):
    split = Mesh(mesh.devices.reshape(4, 4, 8, 2), ("x", "y", "z", "c"))
    whole = ("x", "y", "z", "c")
    return jax.shard_map(
        shards,
        mesh=split,
        in_specs=(P(whole, None), P(whole, None), P(), P(whole, None), P(whole)),
        out_specs=(P(whole), P(whole, None), P(whole, None)),
        check_vma=False,
    )
```

```python
import jax
import jax.numpy as jnp
from jax import lax
from jax.experimental import pallas as pl
from jax.experimental.pallas import tpu as pltpu
from jax.sharding import Mesh, PartitionSpec as P

epsilon = 1e-06
score_scale = 50.0


chunk = 512


def pieces(width):
    return [pl.ds(i, chunk) for i in range(0, width, chunk)]


def fold(value):
    out = value[:, :128]
    for i in range(128, value.shape[1], 128):
        out += value[:, i : i + 128]
    return out


def unit_rows(hidden_ref, gain_ref, part, unit_ref, norm_ref):
    count, width = part.size, hidden_ref.shape[1]
    square = jnp.zeros((count, 128), jnp.float32)
    for at in pieces(width):
        scaled = hidden_ref[part, at].astype(jnp.float32) * gain_ref[:, at]
        square += fold(scaled * scaled)
    norm = jnp.sqrt(jnp.sum(square, axis=-1, keepdims=True) + epsilon)
    inverse = 1.0 / norm
    for at in pieces(width):
        scaled = hidden_ref[part, at].astype(jnp.float32) * gain_ref[:, at]
        unit_ref[part, at] = (scaled * inverse).astype(jnp.bfloat16)
    norm_ref[part, :] = norm


def embed_kernel(hidden_ref, gain_ref, unit_ref, norm_ref):
    for first in range(0, hidden_ref.shape[0], 32):
        unit_rows(hidden_ref, gain_ref, pl.ds(first, 32), unit_ref, norm_ref)


def embed(hidden, gain):
    rows, width = hidden.shape
    vmem = pl.BlockSpec(memory_space=pltpu.VMEM)
    return pl.pallas_call(
        embed_kernel,
        in_specs=[vmem] * 2,
        out_specs=[vmem] * 2,
        out_shape=[
            jax.ShapeDtypeStruct((rows, width), jnp.bfloat16),
            jax.ShapeDtypeStruct((rows, 1), jnp.float32),
        ],
        cost_estimate=pl.CostEstimate(
            flops=4 * rows * width, bytes_accessed=4 * rows * width, transcendentals=0
        ),
    )(hidden, gain[None, :])


low = 64
note_rows = 16


def embed_noted_kernel(
    inside, rows_block, ids_ref, positive_ref, hidden_ref, gain_ref, other_ref, unit_ref, norm_ref, copy_ref
):
    copy_ref[...] = other_ref[...]
    rows, width = hidden_ref.shape
    for first in range(0, rows, 32):
        unit_rows(hidden_ref, gain_ref, pl.ds(first, 32), unit_ref, norm_ref)
    positive = jnp.broadcast_to(positive_ref[...], (note_rows, rows))
    extra = jnp.maximum(positive - inside, 0)
    which, within = extra // rows, extra % rows
    lane_block = lax.broadcasted_iota(jnp.int32, (note_rows, rows), 1) // rows_block
    block = jnp.zeros((note_rows, rows), jnp.int32)
    member = jnp.zeros((note_rows, rows), jnp.int32)
    for k in range(ids_ref.shape[1]):
        block = jnp.where(which == k, ids_ref[0, k], block)
        member = jnp.where(lane_block == ids_ref[0, k], 1, member)
    code = within // rows_block * rows + block * rows_block + within % rows_block
    kind = lax.broadcasted_iota(jnp.int32, (note_rows, rows), 0)
    notes = jnp.where(kind == 0, jnp.where(positive < inside, -1, code // low), 0)
    notes = jnp.where(kind == 1, code % low, jnp.where(kind == 2, member, notes))
    unit_ref[pl.ds(rows, note_rows), :] = jnp.zeros((note_rows, width), jnp.bfloat16)
    unit_ref[pl.ds(rows, note_rows), pl.ds(0, rows)] = notes.astype(jnp.float32).astype(jnp.bfloat16)


def embed_noted(hidden, gain, ids, positive, inside, rows_block, other):
    rows, width = hidden.shape
    vmem = pl.BlockSpec(memory_space=pltpu.VMEM)
    return pl.pallas_call(
        lambda *refs: embed_noted_kernel(inside, rows_block, *refs),
        in_specs=[pl.BlockSpec(memory_space=pltpu.SMEM)]
        + [vmem] * 4,
        out_specs=[vmem] * 3,
        out_shape=[
            jax.ShapeDtypeStruct((rows + note_rows, width), jnp.bfloat16),
            jax.ShapeDtypeStruct((rows, 1), jnp.float32),
            jax.ShapeDtypeStruct(other.shape, other.dtype),
        ],
        cost_estimate=pl.CostEstimate(
            flops=4 * rows * width, bytes_accessed=4 * rows * width, transcendentals=0
        ),
    )(ids, positive[None, :], hidden, gain[None, :], other)


def unembed_kernel(count, gain_ref, norm_ref, *refs):
    sources, out_ref = refs[:count], refs[count]
    here, (made_ref, kept_ref, sems) = refs[count + 1 : -3], refs[-3:]
    rows, width = made_ref.shape
    height = kept_ref.shape[0]
    parts = [pl.ds(first, height) for first in range(0, rows, height)]
    into = [
        [
            pltpu.make_async_copy(source.at[part, :], held.at[part, :], sems.at[k, i])
            for k, (source, held) in enumerate(zip(sources, here))
        ]
        for i, part in enumerate(parts)
    ]
    back = [
        pltpu.make_async_copy(made_ref.at[part, :], out_ref.at[part, :], sems.at[count, i])
        for i, part in enumerate(parts)
    ]
    for copies in into:
        for copy in copies:
            copy.start()
    for i, part in enumerate(parts):
        for copy in into[i]:
            copy.wait()
        inverse = 1.0 / norm_ref[part, :]
        inner = jnp.zeros((height, 128), jnp.float32)
        for at in pieces(width):
            grads = here[1][part, at].astype(jnp.float32)
            for ref in here[2:]:
                grads += ref[part, at].astype(jnp.float32)
            kept_ref[:, at] = grads
            unit = here[0][part, at].astype(jnp.float32) * gain_ref[:, at]
            inner += fold(unit * grads)
        inner = jnp.sum(inner, axis=-1, keepdims=True) * inverse
        for at in pieces(width):
            unit = here[0][part, at].astype(jnp.float32) * gain_ref[:, at] * inverse
            grads = kept_ref[:, at] - unit * inner
            made_ref[part, at] = (grads * (score_scale * inverse) * gain_ref[:, at]).astype(
                jnp.bfloat16
            )
        back[i].start()
    for copy in back:
        copy.wait()


def unembed(hidden, gain, norms, terms):
    rows, width = hidden.shape
    vmem = pl.BlockSpec(memory_space=pltpu.VMEM)
    anywhere = pl.BlockSpec(memory_space=pl.ANY)
    count = 1 + len(terms)
    return pl.pallas_call(
        lambda *refs: unembed_kernel(count, *refs),
        in_specs=[vmem] * 2 + [anywhere] * count,
        out_specs=anywhere,
        out_shape=jax.ShapeDtypeStruct((rows, width), jnp.bfloat16),
        scratch_shapes=[pltpu.VMEM((rows, width), a.dtype) for a in (hidden, *terms)]
        + [
            pltpu.VMEM((rows, width), jnp.bfloat16),
            pltpu.VMEM((32, width), jnp.float32),
            pltpu.SemaphoreType.DMA((count + 1, rows // 32)),
        ],
        compiler_params=pltpu.CompilerParams(vmem_limit_bytes=60 * 1024 * 1024),
        cost_estimate=pl.CostEstimate(
            flops=8 * rows * width, bytes_accessed=8 * rows * width, transcendentals=0
        ),
    )(gain[None, :], norms, hidden, *terms)


def scores_kernel(passage_ref, query_ref, member_ref, code_ref, base_ref, powers_ref, sums_ref):
    step, rows = pl.program_id(0), member_ref.shape[0]

    @pl.when(step == 0)
    def _():
        sums_ref[...] = jnp.zeros_like(sums_ref)

    height = 2 * rows
    slots = passage_ref.shape[0] // rows
    row = lax.broadcasted_iota(jnp.int32, (rows, code_ref.shape[1]), 0)
    total, target_score = sums_ref[0:1, :], sums_ref[1:2, :]
    for pair in range(passage_ref.shape[0] // height):
        both = score_scale * jnp.dot(
            passage_ref[pl.ds(pair * height, height), :],
            query_ref[...],
            preferred_element_type=jnp.float32,
        )
        for j in range(2):
            scores = both[j * rows : (j + 1) * rows]
            slot = 2 * pair + j
            powers = jnp.where(member_ref[...] > 0, jnp.exp(scores), 0.0)
            target = code_ref[...] == row + base_ref[step * slots + slot]
            powers_ref[pl.ds(slot * rows, rows), :] = powers
            total = total + jnp.sum(powers, axis=0, keepdims=True)
            target_score = target_score + jnp.sum(
                jnp.where(target, scores, 0.0), axis=0, keepdims=True
            )
    sums_ref[0:1, :] = total
    sums_ref[1:2, :] = target_score


def score(passages, queries, members, codes, bases):
    count, width = passages.shape
    total, tile = queries.shape[1], count // 4
    return pl.pallas_call(
        scores_kernel,
        grid=(count // tile,),
        in_specs=[
            pl.BlockSpec((tile, width), lambda i: (i, 0)),
            pl.BlockSpec(memory_space=pltpu.VMEM),
            pl.BlockSpec(members.shape, lambda i: (0, 0)),
            pl.BlockSpec((1, total), lambda i: (0, 0)),
            pl.BlockSpec(memory_space=pltpu.SMEM),
        ],
        out_specs=[
            pl.BlockSpec((tile, total), lambda i: (i, 0)),
            pl.BlockSpec((8, total), lambda i: (0, 0)),
        ],
        out_shape=[
            jax.ShapeDtypeStruct((count, total), jnp.float32),
            jax.ShapeDtypeStruct((8, total), jnp.float32),
        ],
        compiler_params=pltpu.CompilerParams(vmem_limit_bytes=50 * 1024 * 1024),
        cost_estimate=pl.CostEstimate(
            flops=2 * count * total * width,
            bytes_accessed=2 * (count + total) * width,
            transcendentals=count * total,
        ),
    )(passages, queries, members, codes, bases)


def spread_kernel(powers_ref, scale_ref, code_ref, base_ref, query_ref, weights_ref, out_ref):
    @pl.when(pl.program_id(0) == 0)
    def _():
        strip = 128
        for j in range(powers_ref.shape[0] // strip):
            part = pl.ds(j * strip, strip)
            row = lax.broadcasted_iota(jnp.int32, (strip, powers_ref.shape[1]), 0)
            target = (code_ref[...] == row + base_ref[j]).astype(jnp.float32)
            weights_ref[part, :] = (powers_ref[part, :] * scale_ref[...] - target).astype(
                jnp.bfloat16
            )

    out_ref[...] = jnp.dot(
        weights_ref[...], query_ref[...], preferred_element_type=jnp.float32
    ).astype(jnp.bfloat16)


def spread(powers, scale, codes, bases, queries):
    count, total = powers.shape
    width, tile = queries.shape[1], 512
    whole = pl.BlockSpec((count, total), lambda i: (0, 0))
    line = pl.BlockSpec((1, total), lambda i: (0, 0))
    return pl.pallas_call(
        spread_kernel,
        grid=(width // tile,),
        in_specs=[
            whole,
            line,
            line,
            pl.BlockSpec(memory_space=pltpu.SMEM),
            pl.BlockSpec((total, tile), lambda i: (0, i)),
        ],
        out_specs=[whole, pl.BlockSpec((count, tile), lambda i: (0, i))],
        out_shape=[
            jax.ShapeDtypeStruct((count, total), jnp.bfloat16),
            jax.ShapeDtypeStruct((count, width), jnp.bfloat16),
        ],
        compiler_params=pltpu.CompilerParams(vmem_limit_bytes=60 * 1024 * 1024),
        cost_estimate=pl.CostEstimate(
            flops=2 * count * total * width,
            bytes_accessed=2 * (count + total) * width,
            transcendentals=0,
        ),
    )(powers, scale, codes, bases, queries)


def gated_kernel(first, value_ref, *refs):
    refs[-1][...] = value_ref[pl.ds(first, refs[-1].shape[0]), :]


def gated(value, *others, rows=None):
    first, count = rows or (0, value.shape[0])
    return pl.pallas_call(
        lambda *refs: gated_kernel(first, *refs),
        in_specs=[pl.BlockSpec(memory_space=pltpu.VMEM)]
        + [pl.BlockSpec(memory_space=pl.ANY)] * len(others),
        out_specs=pl.BlockSpec(memory_space=pltpu.VMEM),
        out_shape=jax.ShapeDtypeStruct((count, *value.shape[1:]), value.dtype),
    )(value, *others)


def shift(value, axis, by):
    size = lax.axis_size(axis)
    return lax.ppermute(value, axis, [(i, (i + by) % size) for i in range(size)])


def offsets(size):
    far = size // 2
    return [far] + [s * k for k in range(far - 1, 0, -1) for s in (1, -1)] + [0]


def sum_over(value, axis, order, dim):
    size = lax.axis_size(axis)
    place = {k % size: j for j, k in enumerate(order)}
    by = size // 2
    while by:
        other = shift(value, axis, -by)
        moved = [
            lax.index_in_dim(other, place[(k - by) % size], dim, keepdims=True) for k in order
        ]
        value = value + jnp.concatenate(moved, axis=dim)
        by //= 2
    return value


def ring_gather(own, axis, cut, copy=None):
    half = lax.axis_size(axis) // 2
    blocks = {0: own}
    up, down = own, own if copy is None else copy
    for step in range(1, half):
        up, down = shift(up, axis, 1), shift(down, axis, -1)
        blocks[-step], blocks[step] = up, down
    blocks[half] = jnp.concatenate([shift(up[:cut], axis, 1), shift(down[cut:], axis, -1)], axis=0)
    return blocks


def ring_scatter(terms, axis):
    half = lax.axis_size(axis) // 2
    arrived = []
    far = terms[half](arrived).astype(jnp.bfloat16)
    rows = far.shape[0] // 2
    up, down = shift(far[:rows], axis, 1), shift(far[rows:], axis, -1)
    for step in range(half - 1, 0, -1):
        arrived.append((up, down))
        above, below = (terms[k](arrived).astype(jnp.float32) for k in (step, -step))
        if step == half - 1:
            up = jnp.concatenate([above[:rows] + up, above[rows:]], axis=0)
            down = jnp.concatenate([below[:rows], below[rows:] + down], axis=0)
        else:
            up, down = above + up, below + down
        up = shift(up.astype(jnp.bfloat16), axis, 1)
        down = shift(down.astype(jnp.bfloat16), axis, -1)
    return terms[0](arrived), up, down


def dot(a, b, dims, kind=jnp.float32):
    return lax.dot_general(a, b, (dims, ((), ())), preferred_element_type=jnp.float32).astype(kind)


def shards(query_hidden, passage_hidden, gain, block_ids, positive_ids):
    groups, n_y, n_z, n_c = (lax.axis_size(a) for a in ("x", "y", "z", "c"))
    i_x, i_y, i_c = (lax.axis_index(a) for a in ("x", "y", "c"))
    sources = n_y * n_z * n_c
    rows, width = query_hidden.shape
    rows_block = rows // sources
    inside = groups * rows
    x_order, y_order = offsets(groups), offsets(n_y)
    blocks = n_c * n_y
    own = n_y - 1

    passage_unit, passage_norms = embed(passage_hidden, gain)
    passages = lax.all_gather(passage_unit, "z", axis=0, tiled=True)
    slots = (i_y * n_z + jnp.arange(n_z)) * n_c + i_c

    noted, query_norms, copy = embed_noted(
        query_hidden, gain, block_ids, positive_ids, inside, rows_block, passage_unit
    )
    row = ring_gather(noted, "y", rows // 2)
    row = [row[k] for k in y_order]
    row = row + [shift(b, "c", 1) for b in row]
    query_unit = noted[:rows]
    queries = jnp.concatenate([b[:rows] for b in row], axis=0)
    notes = jnp.stack([b[rows : rows + 3, :rows] for b in row]).astype(jnp.int32)
    codes = (notes[:, 0] * low + notes[:, 1]).reshape(1, blocks * rows)
    members = jnp.repeat(notes[:, 2].T, rows, axis=1)

    inbatch = ring_gather(passage_unit, "x", rows // 2, copy)
    inbatch = jnp.concatenate([inbatch[k] for k in x_order], axis=0)
    x_slots = (i_x + jnp.array(x_order)) % groups
    inbatch_code = (x_slots[:, None] * rows + jnp.arange(rows)[None, :]).reshape(-1)
    scores_in = score_scale * dot(query_unit, inbatch, ((1,), (1,)))
    target_in = inbatch_code[None, :] == positive_ids[:, None]
    powers_in = jnp.exp(scores_in)
    own_sums = jnp.stack(
        [jnp.sum(powers_in, axis=1), jnp.sum(jnp.where(target_in, scores_in, 0.0), axis=1)]
    )

    members = members.astype(jnp.float32)
    across = lax.optimization_barrier(queries.T)
    powers, sums = score(passages, across, members, codes, slots * rows)
    sums = sums[:2]
    sums = sums + jnp.pad(own_sums, ((0, 0), (own * rows, (blocks - 1 - own) * rows)))
    sums = sums.reshape(2, n_c, n_y, rows)
    sums = sums + shift(sums, "c", 1)[:, ::-1]
    sums = sum_over(sums, "y", y_order, 2).reshape(2, blocks * rows)
    scale = 1.0 / sums[:1]

    weights, passage_part = spread(powers, scale, codes, slots * rows, queries)
    fetched = lax.psum_scatter(passage_part, "z", scatter_dimension=0, tiled=True)

    half = n_y * rows
    there = dot(weights[:, half:], passages, ((0,), (0,)), jnp.bfloat16)
    here = dot(weights[:, :half], passages, ((0,), (0,))) + shift(there, "c", 1).astype(jnp.float32)
    here = here.astype(jnp.bfloat16).reshape(n_y, rows, width)
    query_terms = ring_scatter({k: (lambda _, j=j: here[j]) for j, k in enumerate(y_order)}, "y")

    own_sums = sums[:, own * rows : (own + 1) * rows]
    losses = jnp.log(own_sums[0]) - own_sums[1]
    scale_in = gated(1.0 / own_sums[:1], weights)[0]
    weights_in = lax.optimization_barrier(
        (powers_in * scale_in[:, None] - target_in.astype(jnp.float32)).astype(jnp.bfloat16)
    )
    inside_grad = dot(weights_in, query_unit, ((0,), (0,)), jnp.bfloat16)
    inside_grad = inside_grad.reshape(groups, rows, width)
    inside_terms = ring_scatter(
        {k: (lambda _, j=j: inside_grad[j]) for j, k in enumerate(x_order)}, "x"
    )
    inside_query = dot(weights_in, inbatch, ((1,), (0,)))

    query_grad = unembed(query_hidden, gain, query_norms, (*query_terms, inside_query))
    passage_grad = unembed(passage_hidden, gain, passage_norms, (fetched, *inside_terms))
    return (losses, query_grad, passage_grad)


def solution(mesh):
    split = Mesh(mesh.devices.reshape(4, 4, 8, 2), ("x", "y", "z", "c"))
    whole = ("x", "y", "z", "c")
    return jax.shard_map(
        shards,
        mesh=split,
        in_specs=(P(whole, None), P(whole, None), P(), P(whole, None), P(whole)),
        out_specs=(P(whole), P(whole, None), P(whole, None)),
        check_vma=False,
    )
```

```python
import jax
import jax.numpy as jnp
from jax import lax
from jax.experimental import pallas as pl
from jax.experimental.pallas import tpu as pltpu
from jax.sharding import Mesh, PartitionSpec as P

epsilon = 1e-06
score_scale = 50.0


chunk = 512


def pieces(width):
    return [pl.ds(i, chunk) for i in range(0, width, chunk)]


def fold(value):
    out = value[:, :128]
    for i in range(128, value.shape[1], 128):
        out += value[:, i : i + 128]
    return out


def unit_rows(hidden_ref, gain_ref, part, unit_ref, norm_ref):
    count, width = part.size, hidden_ref.shape[1]
    square = jnp.zeros((count, 128), jnp.float32)
    for at in pieces(width):
        scaled = hidden_ref[part, at].astype(jnp.float32) * gain_ref[:, at]
        square += fold(scaled * scaled)
    norm = jnp.sqrt(jnp.sum(square, axis=-1, keepdims=True) + epsilon)
    inverse = 1.0 / norm
    for at in pieces(width):
        scaled = hidden_ref[part, at].astype(jnp.float32) * gain_ref[:, at]
        unit_ref[part, at] = (scaled * inverse).astype(jnp.bfloat16)
    norm_ref[part, :] = norm


def embed_kernel(hidden_ref, gain_ref, unit_ref, norm_ref):
    for first in range(0, hidden_ref.shape[0], 32):
        unit_rows(hidden_ref, gain_ref, pl.ds(first, 32), unit_ref, norm_ref)


def embed(hidden, gain):
    rows, width = hidden.shape
    vmem = pl.BlockSpec(memory_space=pltpu.VMEM)
    return pl.pallas_call(
        embed_kernel,
        in_specs=[vmem] * 2,
        out_specs=[vmem] * 2,
        out_shape=[
            jax.ShapeDtypeStruct((rows, width), jnp.bfloat16),
            jax.ShapeDtypeStruct((rows, 1), jnp.float32),
        ],
        cost_estimate=pl.CostEstimate(
            flops=4 * rows * width, bytes_accessed=4 * rows * width, transcendentals=0
        ),
    )(hidden, gain[None, :])


low = 64
note_rows = 16


def embed_noted_kernel(
    inside, rows_block, ids_ref, positive_ref, hidden_ref, gain_ref, other_ref, unit_ref, norm_ref, copy_ref
):
    copy_ref[...] = other_ref[...]
    rows, width = hidden_ref.shape
    for first in range(0, rows, 32):
        unit_rows(hidden_ref, gain_ref, pl.ds(first, 32), unit_ref, norm_ref)
    positive = jnp.broadcast_to(positive_ref[...], (note_rows, rows))
    extra = jnp.maximum(positive - inside, 0)
    which, within = extra // rows, extra % rows
    lane_block = lax.broadcasted_iota(jnp.int32, (note_rows, rows), 1) // rows_block
    block = jnp.zeros((note_rows, rows), jnp.int32)
    member = jnp.zeros((note_rows, rows), jnp.int32)
    for k in range(ids_ref.shape[1]):
        block = jnp.where(which == k, ids_ref[0, k], block)
        member = jnp.where(lane_block == ids_ref[0, k], 1, member)
    code = within // rows_block * rows + block * rows_block + within % rows_block
    kind = lax.broadcasted_iota(jnp.int32, (note_rows, rows), 0)
    notes = jnp.where(kind == 0, jnp.where(positive < inside, -1, code // low), 0)
    notes = jnp.where(kind == 1, code % low, jnp.where(kind == 2, member, notes))
    unit_ref[pl.ds(rows, note_rows), :] = jnp.zeros((note_rows, width), jnp.bfloat16)
    unit_ref[pl.ds(rows, note_rows), pl.ds(0, rows)] = notes.astype(jnp.float32).astype(jnp.bfloat16)


def embed_noted(hidden, gain, ids, positive, inside, rows_block, other):
    rows, width = hidden.shape
    vmem = pl.BlockSpec(memory_space=pltpu.VMEM)
    return pl.pallas_call(
        lambda *refs: embed_noted_kernel(inside, rows_block, *refs),
        in_specs=[pl.BlockSpec(memory_space=pltpu.SMEM)]
        + [vmem] * 4,
        out_specs=[vmem] * 3,
        out_shape=[
            jax.ShapeDtypeStruct((rows + note_rows, width), jnp.bfloat16),
            jax.ShapeDtypeStruct((rows, 1), jnp.float32),
            jax.ShapeDtypeStruct(other.shape, other.dtype),
        ],
        cost_estimate=pl.CostEstimate(
            flops=4 * rows * width, bytes_accessed=4 * rows * width, transcendentals=0
        ),
    )(ids, positive[None, :], hidden, gain[None, :], other)


def unembed_kernel(count, gain_ref, norm_ref, *refs):
    sources, out_ref = refs[:count], refs[count]
    here, (made_ref, kept_ref, sems) = refs[count + 1 : -3], refs[-3:]
    rows, width = made_ref.shape
    height = kept_ref.shape[0]
    parts = [pl.ds(first, height) for first in range(0, rows, height)]
    into = [
        [
            pltpu.make_async_copy(source.at[part, :], held.at[part, :], sems.at[k, i])
            for k, (source, held) in enumerate(zip(sources, here))
        ]
        for i, part in enumerate(parts)
    ]
    back = [
        pltpu.make_async_copy(made_ref.at[part, :], out_ref.at[part, :], sems.at[count, i])
        for i, part in enumerate(parts)
    ]
    for copies in into:
        for copy in copies:
            copy.start()
    for i, part in enumerate(parts):
        for copy in into[i]:
            copy.wait()
        inverse = 1.0 / norm_ref[part, :]
        inner = jnp.zeros((height, 128), jnp.float32)
        for at in pieces(width):
            grads = here[1][part, at].astype(jnp.float32)
            for ref in here[2:]:
                grads += ref[part, at].astype(jnp.float32)
            kept_ref[:, at] = grads
            unit = here[0][part, at].astype(jnp.float32) * gain_ref[:, at]
            inner += fold(unit * grads)
        inner = jnp.sum(inner, axis=-1, keepdims=True) * inverse
        for at in pieces(width):
            unit = here[0][part, at].astype(jnp.float32) * gain_ref[:, at] * inverse
            grads = kept_ref[:, at] - unit * inner
            made_ref[part, at] = (grads * (score_scale * inverse) * gain_ref[:, at]).astype(
                jnp.bfloat16
            )
        back[i].start()
    for copy in back:
        copy.wait()


def unembed(hidden, gain, norms, terms):
    rows, width = hidden.shape
    vmem = pl.BlockSpec(memory_space=pltpu.VMEM)
    anywhere = pl.BlockSpec(memory_space=pl.ANY)
    count = 1 + len(terms)
    return pl.pallas_call(
        lambda *refs: unembed_kernel(count, *refs),
        in_specs=[vmem] * 2 + [anywhere] * count,
        out_specs=anywhere,
        out_shape=jax.ShapeDtypeStruct((rows, width), jnp.bfloat16),
        scratch_shapes=[pltpu.VMEM((rows, width), a.dtype) for a in (hidden, *terms)]
        + [
            pltpu.VMEM((rows, width), jnp.bfloat16),
            pltpu.VMEM((32, width), jnp.float32),
            pltpu.SemaphoreType.DMA((count + 1, rows // 32)),
        ],
        compiler_params=pltpu.CompilerParams(vmem_limit_bytes=60 * 1024 * 1024),
        cost_estimate=pl.CostEstimate(
            flops=8 * rows * width, bytes_accessed=8 * rows * width, transcendentals=0
        ),
    )(gain[None, :], norms, hidden, *terms)


def scores_kernel(passage_ref, query_ref, member_ref, code_ref, base_ref, powers_ref, sums_ref):
    step, rows = pl.program_id(0), member_ref.shape[0]

    @pl.when(step == 0)
    def _():
        sums_ref[...] = jnp.zeros_like(sums_ref)

    height = 2 * rows
    slots = passage_ref.shape[0] // rows
    row = lax.broadcasted_iota(jnp.int32, (rows, code_ref.shape[1]), 0)
    total, target_score = sums_ref[0:1, :], sums_ref[1:2, :]
    for pair in range(passage_ref.shape[0] // height):
        both = score_scale * jnp.dot(
            passage_ref[pl.ds(pair * height, height), :],
            query_ref[...],
            preferred_element_type=jnp.float32,
        )
        for j in range(2):
            scores = both[j * rows : (j + 1) * rows]
            slot = 2 * pair + j
            powers = jnp.where(member_ref[...] > 0, jnp.exp(scores), 0.0)
            target = code_ref[...] == row + base_ref[step * slots + slot]
            powers_ref[pl.ds(slot * rows, rows), :] = powers
            total = total + jnp.sum(powers, axis=0, keepdims=True)
            target_score = target_score + jnp.sum(
                jnp.where(target, scores, 0.0), axis=0, keepdims=True
            )
    sums_ref[0:1, :] = total
    sums_ref[1:2, :] = target_score


def score(passages, queries, members, codes, bases):
    count, width = passages.shape
    total, tile = queries.shape[1], count // 4
    return pl.pallas_call(
        scores_kernel,
        grid=(count // tile,),
        in_specs=[
            pl.BlockSpec((tile, width), lambda i: (i, 0)),
            pl.BlockSpec(memory_space=pltpu.VMEM),
            pl.BlockSpec(members.shape, lambda i: (0, 0)),
            pl.BlockSpec((1, total), lambda i: (0, 0)),
            pl.BlockSpec(memory_space=pltpu.SMEM),
        ],
        out_specs=[
            pl.BlockSpec((tile, total), lambda i: (i, 0)),
            pl.BlockSpec((8, total), lambda i: (0, 0)),
        ],
        out_shape=[
            jax.ShapeDtypeStruct((count, total), jnp.float32),
            jax.ShapeDtypeStruct((8, total), jnp.float32),
        ],
        compiler_params=pltpu.CompilerParams(vmem_limit_bytes=52 * 1024 * 1024),
        cost_estimate=pl.CostEstimate(
            flops=2 * count * total * width,
            bytes_accessed=2 * (count + total) * width,
            transcendentals=count * total,
        ),
    )(passages, queries, members, codes, bases)


def spread_kernel(powers_ref, scale_ref, code_ref, base_ref, query_ref, weights_ref, out_ref):
    @pl.when(pl.program_id(0) == 0)
    def _():
        strip = 128
        for j in range(powers_ref.shape[0] // strip):
            part = pl.ds(j * strip, strip)
            row = lax.broadcasted_iota(jnp.int32, (strip, powers_ref.shape[1]), 0)
            target = (code_ref[...] == row + base_ref[j]).astype(jnp.float32)
            weights_ref[part, :] = (powers_ref[part, :] * scale_ref[...] - target).astype(
                jnp.bfloat16
            )

    out_ref[...] = jnp.dot(
        weights_ref[...], query_ref[...], preferred_element_type=jnp.float32
    ).astype(jnp.bfloat16)


def spread(powers, scale, codes, bases, queries):
    count, total = powers.shape
    width, tile = queries.shape[1], 1024
    whole = pl.BlockSpec((count, total), lambda i: (0, 0))
    line = pl.BlockSpec((1, total), lambda i: (0, 0))
    return pl.pallas_call(
        spread_kernel,
        grid=(width // tile,),
        in_specs=[
            whole,
            line,
            line,
            pl.BlockSpec(memory_space=pltpu.SMEM),
            pl.BlockSpec((total, tile), lambda i: (0, i)),
        ],
        out_specs=[whole, pl.BlockSpec((count, tile), lambda i: (0, i))],
        out_shape=[
            jax.ShapeDtypeStruct((count, total), jnp.bfloat16),
            jax.ShapeDtypeStruct((count, width), jnp.bfloat16),
        ],
        compiler_params=pltpu.CompilerParams(vmem_limit_bytes=52 * 1024 * 1024),
        cost_estimate=pl.CostEstimate(
            flops=2 * count * total * width,
            bytes_accessed=2 * (count + total) * width,
            transcendentals=0,
        ),
    )(powers, scale, codes, bases, queries)


def gated_kernel(first, value_ref, *refs):
    refs[-1][...] = value_ref[pl.ds(first, refs[-1].shape[0]), :]


def gated(value, *others, rows=None):
    first, count = rows or (0, value.shape[0])
    return pl.pallas_call(
        lambda *refs: gated_kernel(first, *refs),
        in_specs=[pl.BlockSpec(memory_space=pltpu.VMEM)]
        + [pl.BlockSpec(memory_space=pl.ANY)] * len(others),
        out_specs=pl.BlockSpec(memory_space=pltpu.VMEM),
        out_shape=jax.ShapeDtypeStruct((count, *value.shape[1:]), value.dtype),
    )(value, *others)


def shift(value, axis, by):
    size = lax.axis_size(axis)
    return lax.ppermute(value, axis, [(i, (i + by) % size) for i in range(size)])


def offsets(size):
    far = size // 2
    return [far] + [s * k for k in range(far - 1, 0, -1) for s in (1, -1)] + [0]


def sum_over(value, axis, order, dim):
    size = lax.axis_size(axis)
    place = {k % size: j for j, k in enumerate(order)}
    others = [shift(value, axis, -by) for by in range(1, size)]
    for by, other in enumerate(others, 1):
        moved = [
            lax.index_in_dim(other, place[(k - by) % size], dim, keepdims=True) for k in order
        ]
        value = value + jnp.concatenate(moved, axis=dim)
    return value


def ring_gather(own, axis, cut, copy=None):
    half = lax.axis_size(axis) // 2
    blocks = {0: own}
    up, down = own, own if copy is None else copy
    for step in range(1, half):
        up, down = shift(up, axis, 1), shift(down, axis, -1)
        blocks[-step], blocks[step] = up, down
    blocks[half] = jnp.concatenate([shift(up[:cut], axis, 1), shift(down[cut:], axis, -1)], axis=0)
    return blocks


def ring_scatter(terms, axis):
    half = lax.axis_size(axis) // 2
    arrived = []
    far = terms[half](arrived).astype(jnp.bfloat16)
    rows = far.shape[0] // 2
    up, down = shift(far[:rows], axis, 1), shift(far[rows:], axis, -1)
    for step in range(half - 1, 0, -1):
        arrived.append((up, down))
        above, below = (terms[k](arrived).astype(jnp.float32) for k in (step, -step))
        if step == half - 1:
            up = jnp.concatenate([above[:rows] + up, above[rows:]], axis=0)
            down = jnp.concatenate([below[:rows], below[rows:] + down], axis=0)
        else:
            up, down = above + up, below + down
        up = shift(up.astype(jnp.bfloat16), axis, 1)
        down = shift(down.astype(jnp.bfloat16), axis, -1)
    return terms[0](arrived), up, down


def dot(a, b, dims, kind=jnp.float32):
    return lax.dot_general(a, b, (dims, ((), ())), preferred_element_type=jnp.float32).astype(kind)


def shards(query_hidden, passage_hidden, gain, block_ids, positive_ids):
    groups, n_y, n_z, n_c = (lax.axis_size(a) for a in ("x", "y", "z", "c"))
    i_x, i_y, i_c = (lax.axis_index(a) for a in ("x", "y", "c"))
    sources = n_y * n_z * n_c
    rows, width = query_hidden.shape
    rows_block = rows // sources
    inside = groups * rows
    x_order, y_order = offsets(groups), offsets(n_y)
    blocks = n_c * n_y
    own = n_y - 1

    passage_unit, passage_norms = embed(passage_hidden, gain)
    passages = lax.all_gather(passage_unit, "z", axis=0, tiled=True)
    slots = (i_y * n_z + jnp.arange(n_z)) * n_c + i_c

    noted, query_norms, copy = embed_noted(
        query_hidden, gain, block_ids, positive_ids, inside, rows_block, passage_unit
    )
    row = ring_gather(noted, "y", rows // 2)
    row = [row[k] for k in y_order]
    row = row + [shift(b, "c", 1) for b in row]
    query_unit = noted[:rows]
    queries = jnp.concatenate([b[:rows] for b in row], axis=0)
    notes = jnp.stack([b[rows : rows + 3, :rows] for b in row]).astype(jnp.int32)
    codes = (notes[:, 0] * low + notes[:, 1]).reshape(1, blocks * rows)
    members = jnp.repeat(notes[:, 2].T, rows, axis=1)

    inbatch = ring_gather(passage_unit, "x", rows // 2, copy)
    inbatch = jnp.concatenate([inbatch[k] for k in x_order], axis=0)
    x_slots = (i_x + jnp.array(x_order)) % groups
    inbatch_code = (x_slots[:, None] * rows + jnp.arange(rows)[None, :]).reshape(-1)
    scores_in = score_scale * dot(query_unit, inbatch, ((1,), (1,)))
    target_in = inbatch_code[None, :] == positive_ids[:, None]
    powers_in = jnp.exp(scores_in)
    own_sums = jnp.stack(
        [jnp.sum(powers_in, axis=1), jnp.sum(jnp.where(target_in, scores_in, 0.0), axis=1)]
    )

    members = members.astype(jnp.float32)
    across = lax.optimization_barrier(queries.T)
    powers, sums = score(passages, across, members, codes, slots * rows)
    sums = sums[:2]
    sums = sums + jnp.pad(own_sums, ((0, 0), (own * rows, (blocks - 1 - own) * rows)))
    sums = sums.reshape(2, n_c, n_y, rows)
    sums = sums + shift(sums, "c", 1)[:, ::-1]
    sums = sum_over(sums, "y", y_order, 2).reshape(2, blocks * rows)
    scale = 1.0 / sums[:1]

    weights, passage_part = spread(powers, scale, codes, slots * rows, queries)
    fetched = lax.psum_scatter(passage_part, "z", scatter_dimension=0, tiled=True)

    half = n_y * rows
    there = dot(weights[:, half:], passages, ((0,), (0,)), jnp.bfloat16)
    here = dot(weights[:, :half], passages, ((0,), (0,))) + shift(there, "c", 1).astype(jnp.float32)
    here = here.astype(jnp.bfloat16).reshape(n_y, rows, width)
    query_terms = ring_scatter({k: (lambda _, j=j: here[j]) for j, k in enumerate(y_order)}, "y")

    own_sums = sums[:, own * rows : (own + 1) * rows]
    losses = jnp.log(own_sums[0]) - own_sums[1]
    scale_in = gated(1.0 / own_sums[:1], weights)[0]
    weights_in = lax.optimization_barrier(
        (powers_in * scale_in[:, None] - target_in.astype(jnp.float32)).astype(jnp.bfloat16)
    )
    inside_grad = dot(weights_in, query_unit, ((0,), (0,)), jnp.bfloat16)
    inside_grad = inside_grad.reshape(groups, rows, width)
    inside_terms = ring_scatter(
        {k: (lambda _, j=j: inside_grad[j]) for j, k in enumerate(x_order)}, "x"
    )
    inside_query = dot(weights_in, inbatch, ((1,), (0,)))

    query_grad = unembed(query_hidden, gain, query_norms, (*query_terms, inside_query))
    passage_grad = unembed(passage_hidden, gain, passage_norms, (fetched, *inside_terms))
    return (losses, query_grad, passage_grad)


def solution(mesh):
    split = Mesh(mesh.devices.reshape(4, 4, 8, 2), ("x", "y", "z", "c"))
    whole = ("x", "y", "z", "c")
    return jax.shard_map(
        shards,
        mesh=split,
        in_specs=(P(whole, None), P(whole, None), P(), P(whole, None), P(whole)),
        out_specs=(P(whole), P(whole, None), P(whole, None)),
        check_vma=False,
    )
```

```python
import jax
import jax.numpy as jnp
from jax import lax
from jax.experimental import pallas as pl
from jax.experimental.pallas import tpu as pltpu
from jax.sharding import Mesh, PartitionSpec as P

epsilon = 1e-06
score_scale = 50.0


chunk = 512


def pieces(width):
    return [pl.ds(i, chunk) for i in range(0, width, chunk)]


def fold(value):
    out = value[:, :128]
    for i in range(128, value.shape[1], 128):
        out += value[:, i : i + 128]
    return out


def unit_rows(hidden_ref, gain_ref, part, unit_ref, norm_ref):
    count, width = part.size, hidden_ref.shape[1]
    square = jnp.zeros((count, 128), jnp.float32)
    for at in pieces(width):
        scaled = hidden_ref[part, at].astype(jnp.float32) * gain_ref[:, at]
        square += fold(scaled * scaled)
    norm = jnp.sqrt(jnp.sum(square, axis=-1, keepdims=True) + epsilon)
    inverse = 1.0 / norm
    for at in pieces(width):
        scaled = hidden_ref[part, at].astype(jnp.float32) * gain_ref[:, at]
        unit_ref[part, at] = (scaled * inverse).astype(jnp.bfloat16)
    norm_ref[part, :] = norm


def embed_kernel(hidden_ref, gain_ref, unit_ref, norm_ref):
    for first in range(0, hidden_ref.shape[0], 32):
        unit_rows(hidden_ref, gain_ref, pl.ds(first, 32), unit_ref, norm_ref)


def embed(hidden, gain):
    rows, width = hidden.shape
    vmem = pl.BlockSpec(memory_space=pltpu.VMEM)
    return pl.pallas_call(
        embed_kernel,
        in_specs=[vmem] * 2,
        out_specs=[vmem] * 2,
        out_shape=[
            jax.ShapeDtypeStruct((rows, width), jnp.bfloat16),
            jax.ShapeDtypeStruct((rows, 1), jnp.float32),
        ],
        cost_estimate=pl.CostEstimate(
            flops=4 * rows * width, bytes_accessed=4 * rows * width, transcendentals=0
        ),
    )(hidden, gain[None, :])


low = 64
note_rows = 16


def embed_noted_kernel(
    inside, rows_block, ids_ref, positive_ref, hidden_ref, gain_ref, other_ref, unit_ref, norm_ref, copy_ref
):
    copy_ref[...] = other_ref[...]
    rows, width = hidden_ref.shape
    for first in range(0, rows, 32):
        unit_rows(hidden_ref, gain_ref, pl.ds(first, 32), unit_ref, norm_ref)
    positive = jnp.broadcast_to(positive_ref[...], (note_rows, rows))
    extra = jnp.maximum(positive - inside, 0)
    which, within = extra // rows, extra % rows
    lane_block = lax.broadcasted_iota(jnp.int32, (note_rows, rows), 1) // rows_block
    block = jnp.zeros((note_rows, rows), jnp.int32)
    member = jnp.zeros((note_rows, rows), jnp.int32)
    for k in range(ids_ref.shape[1]):
        block = jnp.where(which == k, ids_ref[0, k], block)
        member = jnp.where(lane_block == ids_ref[0, k], 1, member)
    code = within // rows_block * rows + block * rows_block + within % rows_block
    kind = lax.broadcasted_iota(jnp.int32, (note_rows, rows), 0)
    notes = jnp.where(kind == 0, jnp.where(positive < inside, -1, code // low), 0)
    notes = jnp.where(kind == 1, code % low, jnp.where(kind == 2, member, notes))
    unit_ref[pl.ds(rows, note_rows), :] = jnp.zeros((note_rows, width), jnp.bfloat16)
    unit_ref[pl.ds(rows, note_rows), pl.ds(0, rows)] = notes.astype(jnp.float32).astype(jnp.bfloat16)


def embed_noted(hidden, gain, ids, positive, inside, rows_block, other):
    rows, width = hidden.shape
    vmem = pl.BlockSpec(memory_space=pltpu.VMEM)
    return pl.pallas_call(
        lambda *refs: embed_noted_kernel(inside, rows_block, *refs),
        in_specs=[pl.BlockSpec(memory_space=pltpu.SMEM)]
        + [vmem] * 4,
        out_specs=[vmem] * 3,
        out_shape=[
            jax.ShapeDtypeStruct((rows + note_rows, width), jnp.bfloat16),
            jax.ShapeDtypeStruct((rows, 1), jnp.float32),
            jax.ShapeDtypeStruct(other.shape, other.dtype),
        ],
        cost_estimate=pl.CostEstimate(
            flops=4 * rows * width, bytes_accessed=4 * rows * width, transcendentals=0
        ),
    )(ids, positive[None, :], hidden, gain[None, :], other)


def unembed_kernel(count, gain_ref, norm_ref, *refs):
    sources, out_ref = refs[:count], refs[count]
    here, (made_ref, kept_ref, sems) = refs[count + 1 : -3], refs[-3:]
    rows, width = made_ref.shape
    height = kept_ref.shape[0]
    parts = [pl.ds(first, height) for first in range(0, rows, height)]
    into = [
        [
            pltpu.make_async_copy(source.at[part, :], held.at[part, :], sems.at[k, i])
            for k, (source, held) in enumerate(zip(sources, here))
        ]
        for i, part in enumerate(parts)
    ]
    back = [
        pltpu.make_async_copy(made_ref.at[part, :], out_ref.at[part, :], sems.at[count, i])
        for i, part in enumerate(parts)
    ]
    for copies in into:
        for copy in copies:
            copy.start()
    for i, part in enumerate(parts):
        for copy in into[i]:
            copy.wait()
        inverse = 1.0 / norm_ref[part, :]
        inner = jnp.zeros((height, 128), jnp.float32)
        for at in pieces(width):
            grads = here[1][part, at].astype(jnp.float32)
            for ref in here[2:]:
                grads += ref[part, at].astype(jnp.float32)
            kept_ref[:, at] = grads
            unit = here[0][part, at].astype(jnp.float32) * gain_ref[:, at]
            inner += fold(unit * grads)
        inner = jnp.sum(inner, axis=-1, keepdims=True) * inverse
        for at in pieces(width):
            unit = here[0][part, at].astype(jnp.float32) * gain_ref[:, at] * inverse
            grads = kept_ref[:, at] - unit * inner
            made_ref[part, at] = (grads * (score_scale * inverse) * gain_ref[:, at]).astype(
                jnp.bfloat16
            )
        back[i].start()
    for copy in back:
        copy.wait()


def unembed(hidden, gain, norms, terms):
    rows, width = hidden.shape
    vmem = pl.BlockSpec(memory_space=pltpu.VMEM)
    anywhere = pl.BlockSpec(memory_space=pl.ANY)
    count = 1 + len(terms)
    return pl.pallas_call(
        lambda *refs: unembed_kernel(count, *refs),
        in_specs=[vmem] * 2 + [anywhere] * count,
        out_specs=anywhere,
        out_shape=jax.ShapeDtypeStruct((rows, width), jnp.bfloat16),
        scratch_shapes=[pltpu.VMEM((rows, width), a.dtype) for a in (hidden, *terms)]
        + [
            pltpu.VMEM((rows, width), jnp.bfloat16),
            pltpu.VMEM((32, width), jnp.float32),
            pltpu.SemaphoreType.DMA((count + 1, rows // 32)),
        ],
        compiler_params=pltpu.CompilerParams(vmem_limit_bytes=60 * 1024 * 1024),
        cost_estimate=pl.CostEstimate(
            flops=8 * rows * width, bytes_accessed=8 * rows * width, transcendentals=0
        ),
    )(gain[None, :], norms, hidden, *terms)


def scores_kernel(passage_ref, query_ref, member_ref, code_ref, base_ref, powers_ref, sums_ref):
    step, rows = pl.program_id(0), member_ref.shape[0]

    @pl.when(step == 0)
    def _():
        sums_ref[...] = jnp.zeros_like(sums_ref)

    height = 2 * rows
    slots = passage_ref.shape[0] // rows
    row = lax.broadcasted_iota(jnp.int32, (rows, code_ref.shape[1]), 0)
    total, target_score = sums_ref[0:1, :], sums_ref[1:2, :]
    for pair in range(passage_ref.shape[0] // height):
        both = score_scale * jnp.dot(
            passage_ref[pl.ds(pair * height, height), :],
            query_ref[...],
            preferred_element_type=jnp.float32,
        )
        for j in range(2):
            scores = both[j * rows : (j + 1) * rows]
            slot = 2 * pair + j
            powers = jnp.where(member_ref[...] > 0, jnp.exp(scores), 0.0)
            target = code_ref[...] == row + base_ref[step * slots + slot]
            powers_ref[pl.ds(slot * rows, rows), :] = powers
            total = total + jnp.sum(powers, axis=0, keepdims=True)
            target_score = target_score + jnp.sum(
                jnp.where(target, scores, 0.0), axis=0, keepdims=True
            )
    sums_ref[0:1, :] = total
    sums_ref[1:2, :] = target_score


def score(passages, queries, members, codes, bases):
    count, width = passages.shape
    total, tile = queries.shape[1], count // 4
    return pl.pallas_call(
        scores_kernel,
        grid=(count // tile,),
        in_specs=[
            pl.BlockSpec((tile, width), lambda i: (i, 0)),
            pl.BlockSpec(memory_space=pltpu.VMEM),
            pl.BlockSpec(members.shape, lambda i: (0, 0)),
            pl.BlockSpec((1, total), lambda i: (0, 0)),
            pl.BlockSpec(memory_space=pltpu.SMEM),
        ],
        out_specs=[
            pl.BlockSpec((tile, total), lambda i: (i, 0)),
            pl.BlockSpec((8, total), lambda i: (0, 0)),
        ],
        out_shape=[
            jax.ShapeDtypeStruct((count, total), jnp.float32),
            jax.ShapeDtypeStruct((8, total), jnp.float32),
        ],
        compiler_params=pltpu.CompilerParams(vmem_limit_bytes=52 * 1024 * 1024),
        cost_estimate=pl.CostEstimate(
            flops=2 * count * total * width,
            bytes_accessed=2 * (count + total) * width,
            transcendentals=count * total,
        ),
    )(passages, queries, members, codes, bases)


def spread_kernel(powers_ref, scale_ref, code_ref, base_ref, query_ref, weights_ref, out_ref):
    @pl.when(pl.program_id(0) == 0)
    def _():
        strip = 128
        for j in range(powers_ref.shape[0] // strip):
            part = pl.ds(j * strip, strip)
            row = lax.broadcasted_iota(jnp.int32, (strip, powers_ref.shape[1]), 0)
            target = (code_ref[...] == row + base_ref[j]).astype(jnp.float32)
            weights_ref[part, :] = (powers_ref[part, :] * scale_ref[...] - target).astype(
                jnp.bfloat16
            )

    out_ref[...] = jnp.dot(
        weights_ref[...], query_ref[...], preferred_element_type=jnp.float32
    ).astype(jnp.bfloat16)


def spread(powers, scale, codes, bases, queries):
    count, total = powers.shape
    width, tile = queries.shape[1], 1024
    whole = pl.BlockSpec((count, total), lambda i: (0, 0))
    line = pl.BlockSpec((1, total), lambda i: (0, 0))
    return pl.pallas_call(
        spread_kernel,
        grid=(width // tile,),
        in_specs=[
            whole,
            line,
            line,
            pl.BlockSpec(memory_space=pltpu.SMEM),
            pl.BlockSpec((total, tile), lambda i: (0, i)),
        ],
        out_specs=[whole, pl.BlockSpec((count, tile), lambda i: (0, i))],
        out_shape=[
            jax.ShapeDtypeStruct((count, total), jnp.bfloat16),
            jax.ShapeDtypeStruct((count, width), jnp.bfloat16),
        ],
        compiler_params=pltpu.CompilerParams(vmem_limit_bytes=52 * 1024 * 1024),
        cost_estimate=pl.CostEstimate(
            flops=2 * count * total * width,
            bytes_accessed=2 * (count + total) * width,
            transcendentals=0,
        ),
    )(powers, scale, codes, bases, queries)


def gated_kernel(first, value_ref, *refs):
    refs[-1][...] = value_ref[pl.ds(first, refs[-1].shape[0]), :]


def gated(value, *others, rows=None):
    first, count = rows or (0, value.shape[0])
    return pl.pallas_call(
        lambda *refs: gated_kernel(first, *refs),
        in_specs=[pl.BlockSpec(memory_space=pltpu.VMEM)]
        + [pl.BlockSpec(memory_space=pl.ANY)] * len(others),
        out_specs=pl.BlockSpec(memory_space=pltpu.VMEM),
        out_shape=jax.ShapeDtypeStruct((count, *value.shape[1:]), value.dtype),
    )(value, *others)


def shift(value, axis, by):
    size = lax.axis_size(axis)
    return lax.ppermute(value, axis, [(i, (i + by) % size) for i in range(size)])


def offsets(size):
    far = size // 2
    return [far] + [s * k for k in range(far - 1, 0, -1) for s in (1, -1)] + [0]


def sum_over(value, axis, order, dim):
    size = lax.axis_size(axis)
    place = {k % size: j for j, k in enumerate(order)}
    others = [shift(value, axis, -by) for by in range(1, size)]
    for by, other in enumerate(others, 1):
        moved = [
            lax.index_in_dim(other, place[(k - by) % size], dim, keepdims=True) for k in order
        ]
        value = value + jnp.concatenate(moved, axis=dim)
    return value


def ring_gather(own, axis, cut, copy=None):
    half = lax.axis_size(axis) // 2
    blocks = {0: own}
    up, down = own, own if copy is None else copy
    for step in range(1, half):
        up, down = shift(up, axis, 1), shift(down, axis, -1)
        blocks[-step], blocks[step] = up, down
    blocks[half] = jnp.concatenate([shift(up[:cut], axis, 1), shift(down[cut:], axis, -1)], axis=0)
    return blocks


def ring_scatter(terms, axis):
    half = lax.axis_size(axis) // 2
    arrived = []
    far = terms[half](arrived).astype(jnp.bfloat16)
    rows = far.shape[0] // 2
    up, down = shift(far[:rows], axis, 1), shift(far[rows:], axis, -1)
    for step in range(half - 1, 0, -1):
        arrived.append((up, down))
        above, below = (terms[k](arrived).astype(jnp.float32) for k in (step, -step))
        if step == half - 1:
            up = jnp.concatenate([above[:rows] + up, above[rows:]], axis=0)
            down = jnp.concatenate([below[:rows], below[rows:] + down], axis=0)
        else:
            up, down = above + up, below + down
        up = shift(up.astype(jnp.bfloat16), axis, 1)
        down = shift(down.astype(jnp.bfloat16), axis, -1)
    return terms[0](arrived), up, down


def dot(a, b, dims, kind=jnp.float32):
    return lax.dot_general(a, b, (dims, ((), ())), preferred_element_type=jnp.float32).astype(kind)


def shards(query_hidden, passage_hidden, gain, block_ids, positive_ids):
    groups, n_y, n_z, n_c = (lax.axis_size(a) for a in ("x", "y", "z", "c"))
    i_x, i_y, i_c = (lax.axis_index(a) for a in ("x", "y", "c"))
    sources = n_y * n_z * n_c
    rows, width = query_hidden.shape
    rows_block = rows // sources
    inside = groups * rows
    x_order, y_order = offsets(groups), offsets(n_y)
    blocks = n_c * n_y
    own = n_y - 1

    passage_unit, passage_norms = embed(passage_hidden, gain)
    passages = lax.all_gather(passage_unit, "z", axis=0, tiled=True)
    slots = (i_y * n_z + jnp.arange(n_z)) * n_c + i_c

    noted, query_norms, copy = embed_noted(
        query_hidden, gain, block_ids, positive_ids, inside, rows_block, passage_unit
    )
    row = ring_gather(noted, "y", rows // 2)
    row = [row[k] for k in y_order]
    row = row + [shift(b, "c", 1) for b in row]
    query_unit = noted[:rows]
    queries = jnp.concatenate([b[:rows] for b in row], axis=0)
    notes = jnp.stack([b[rows : rows + 3, :rows] for b in row]).astype(jnp.int32)
    codes = (notes[:, 0] * low + notes[:, 1]).reshape(1, blocks * rows)
    members = jnp.repeat(notes[:, 2].T, rows, axis=1)

    inbatch = ring_gather(passage_unit, "x", rows // 2, copy)
    inbatch = jnp.concatenate([inbatch[k] for k in x_order], axis=0)
    x_slots = (i_x + jnp.array(x_order)) % groups
    inbatch_code = (x_slots[:, None] * rows + jnp.arange(rows)[None, :]).reshape(-1)
    scores_in = score_scale * dot(query_unit, inbatch, ((1,), (1,)))
    target_in = inbatch_code[None, :] == positive_ids[:, None]
    powers_in = jnp.exp(scores_in)
    own_sums = jnp.stack(
        [jnp.sum(powers_in, axis=1), jnp.sum(jnp.where(target_in, scores_in, 0.0), axis=1)]
    )

    members = members.astype(jnp.float32)
    across = pltpu.with_memory_space_constraint(lax.optimization_barrier(queries.T), pltpu.VMEM)
    powers, sums = score(passages, across, members, codes, slots * rows)
    sums = sums[:2]
    sums = sums + jnp.pad(own_sums, ((0, 0), (own * rows, (blocks - 1 - own) * rows)))
    sums = sums.reshape(2, n_c, n_y, rows)
    sums = sums + shift(sums, "c", 1)[:, ::-1]
    sums = sum_over(sums, "y", y_order, 2).reshape(2, blocks * rows)
    scale = 1.0 / sums[:1]

    weights, passage_part = spread(powers, scale, codes, slots * rows, queries)
    fetched = lax.psum_scatter(passage_part, "z", scatter_dimension=0, tiled=True)

    half = n_y * rows
    there = dot(weights[:, half:], passages, ((0,), (0,)), jnp.bfloat16)
    here = dot(weights[:, :half], passages, ((0,), (0,))) + shift(there, "c", 1).astype(jnp.float32)
    here = here.astype(jnp.bfloat16).reshape(n_y, rows, width)
    query_terms = ring_scatter({k: (lambda _, j=j: here[j]) for j, k in enumerate(y_order)}, "y")

    own_sums = sums[:, own * rows : (own + 1) * rows]
    losses = jnp.log(own_sums[0]) - own_sums[1]
    scale_in = gated(1.0 / own_sums[:1], weights)[0]
    weights_in = lax.optimization_barrier(
        (powers_in * scale_in[:, None] - target_in.astype(jnp.float32)).astype(jnp.bfloat16)
    )
    inside_grad = dot(weights_in, query_unit, ((0,), (0,)), jnp.bfloat16)
    inside_grad = inside_grad.reshape(groups, rows, width)
    inside_terms = ring_scatter(
        {k: (lambda _, j=j: inside_grad[j]) for j, k in enumerate(x_order)}, "x"
    )
    inside_query = dot(weights_in, inbatch, ((1,), (0,)))

    query_grad = unembed(query_hidden, gain, query_norms, (*query_terms, inside_query))
    passage_grad = unembed(passage_hidden, gain, passage_norms, (fetched, *inside_terms))
    return (losses, query_grad, passage_grad)


def solution(mesh):
    split = Mesh(mesh.devices.reshape(4, 4, 8, 2), ("x", "y", "z", "c"))
    whole = ("x", "y", "z", "c")
    return jax.shard_map(
        shards,
        mesh=split,
        in_specs=(P(whole, None), P(whole, None), P(), P(whole, None), P(whole)),
        out_specs=(P(whole), P(whole, None), P(whole, None)),
        check_vma=False,
    )
```
